32 devices in a mesh: expert: 8 (over z, y), shard: 4 (over x, core).
Axes of the slice: x: 2, y: 2, z: 4, core: 2. Of those that a mesh axis runs over, the one named last changes fastest.
Arguments:
- tokens: bfloat16 [5120, 2048], P('expert'), may hold values from -6 to 6
- norm_attn: bfloat16 [2048], replicated, may hold values from 0.5 to 1.5
- w_query: bfloat16 [2048, 2048], P('expert', 'shard'), may hold values from -0.125 to 0.125
- b_query: bfloat16 [2048], replicated, may hold values from -3 to 3
- w_key: bfloat16 [2048, 2048], P('expert', 'shard'), may hold values from -0.125 to 0.125
- b_key: bfloat16 [2048], replicated, may hold values from -3 to 3
- w_value: bfloat16 [2048, 2048], P('expert', 'shard'), may hold values from -0.125 to 0.125
- b_value: bfloat16 [2048], replicated, may hold values from -3 to 3
- w_output: bfloat16 [2048, 2048], P('shard', 'expert'), may hold values from -1 to 1
- norm_ffn: bfloat16 [2048], replicated, may hold values from 0.5 to 1.5
- w_router: bfloat16 [2048, 8], replicated, may hold values from -0.0625 to 0.0625
- shared_mix: bfloat16 [2048], replicated, may hold values from -0.125 to 0.125
- shared_gate: bfloat16 [2048, 5632], P('expert', 'shard'), may hold values from -0.125 to 0.125
- shared_up: bfloat16 [2048, 5632], P('expert', 'shard'), may hold values from -0.125 to 0.125
- shared_down: bfloat16 [5632, 2048], P('shard', 'expert'), may hold values from -0.15625 to 0.15625
- expert_gate: bfloat16 [8, 2048, 1408], P('expert', None, 'shard'), may hold values from -0.125 to 0.125
- expert_up: bfloat16 [8, 2048, 1408], P('expert', None, 'shard'), may hold values from -0.125 to 0.125
- expert_down: bfloat16 [8, 1408, 2048], P('expert', 'shard'), may hold values from -1.25 to 1.25
- routes: int32 [5120, 4], P(('expert', 'shard')), may hold values from 0 to 7, all different within a row; in each aligned block of 160 rows (0 to 159, 160 to 319, ...) at most 100 rows name the same one
- seq_lengths: int32 [32, 8], P('expert'), may hold values from 0 to 160, as said below
- cotangent: bfloat16 [5120, 2048], P('expert'), may hold values from -6 to 6
Outputs:
- block_out: bfloat16 [5120, 2048], P(('expert', 'shard'))
- grad_tokens: float32 [5120, 2048], P(('expert', 'shard'))
- grad_norm_attn: float32 [2048], replicated
- grad_w_query: float32 [2048, 2048], P('expert', 'shard')
- grad_b_query: float32 [2048], replicated
- grad_w_key: float32 [2048, 2048], P('expert', 'shard')
- grad_b_key: float32 [2048], replicated
- grad_w_value: float32 [2048, 2048], P('expert', 'shard')
- grad_b_value: float32 [2048], replicated
- grad_w_output: float32 [2048, 2048], P('shard', 'expert')
- grad_norm_ffn: float32 [2048], replicated
- grad_w_router: float32 [2048, 8], replicated
- grad_shared_mix: float32 [2048], replicated
- grad_shared_gate: float32 [2048, 5632], P('expert', 'shard')
- grad_shared_up: float32 [2048, 5632], P('expert', 'shard')
- grad_shared_down: float32 [5632, 2048], P('shard', 'expert')
- grad_expert_gate: float32 [8, 2048, 1408], P('expert', None, 'shard')
- grad_expert_up: float32 [8, 2048, 1408], P('expert', None, 'shard')
- grad_expert_down: float32 [8, 1408, 2048], P('expert', 'shard')
The draws below stay inside these ranges and needn't reach their ends.
Inputs may be any that keep to these rules, and one draw needn't show every extreme that they name: `routes`: A row names 4 different experts; in every aligned block of 160 rows (the rows of one device) no expert is named by more than 100 rows, and one is named by exactly 100 in some block. `seq_lengths`: row d holds the lengths of device block d's sequences in order: they sum to 160, positive ones first and zeros after; in every draw some device holds a single sequence of 160.
All inputs are finite; a program needn't handle non-finite values.
Results may differ from the reference program's by a relative error of at most 0.025.
Values may be sent and summed in bfloat16 or wider, within the bound.
No kernel may reach another device: no remote copies, remote signals or barrier semaphores. Data moves between devices by JAX's collectives and lax.ppermute only.
A program may use at most 256 MiB of HBM per device.

```python
import math
import jax
import jax.numpy as jnp
import numpy as np
from jax import lax

D = 2048
HEADS = 16
HD = 128
SH = 5632
FFE = 1408
TOP = 4
SLOTS = 8
TOK_DEV = 160
HQ = 2048
EXPERTS = 8
CAP = 100
TOKENS = 5120
DEVICES = 32


def draw_seq_lengths(key, part):
    key = jax.random.fold_in(key, 11)
    count_key, whole_key, split_key = jax.random.split(key, 3)
    counts = jax.random.randint(count_key, (DEVICES,), 1, SLOTS + 1)
    single = jax.random.randint(whole_key, (), 0, DEVICES)
    counts = jnp.where(jnp.arange(DEVICES) == single, 1, counts)
    row_keys = jax.random.split(split_key, DEVICES)

    def one_row(row_key, pieces):
        shuffled = jax.random.permutation(row_key, TOK_DEV - 1)[:SLOTS - 1] + 1
        cut_points = jnp.where(jnp.arange(SLOTS - 1) < pieces - 1, shuffled, TOK_DEV)
        cut_points = jnp.sort(cut_points).astype(jnp.int32)
        boundary = jnp.concatenate([jnp.zeros((1,), jnp.int32), cut_points, jnp.full((1,), TOK_DEV, jnp.int32)])
        return boundary[1:] - boundary[:-1]
    return jax.vmap(one_row)(row_keys, counts).astype(jnp.int32)


def level_of(own_key, dims, cuts, least, largest):
    def one(position, blocks):
        draws = jax.random.uniform(jax.random.fold_in(jax.random.fold_in(own_key, 6), position), (blocks,), jnp.float32, least / len(cuts), largest / len(cuts))
        return jnp.repeat(jnp.exp(draws), dims[position] // blocks).reshape((-1,) + (1,) * (len(dims) - position - 1))

    loudness = one(*cuts[0])
    for cut in cuts[1:]:
        loudness = loudness * one(*cut)
    return loudness


def shared_out(own_key, own, number, rows, count, top, bound, skew):
    ranking = jax.random.permutation(own_key, count)
    packed, usual = shares(count, rows * top, bound, skew, True), shares(count, rows * top, bound, skew, False)
    places = jnp.arange(count)

    def named(sizes, offset_by):
        used = int((sizes > 0).sum())
        fixed = max(1, used // 4)
        passed = fixed + (places - fixed + offset_by * (used - fixed)) % max(1, count - fixed)
        return jnp.zeros((count,), jnp.int32).at[ranking[jnp.where(places < fixed, places, passed)]].set(jnp.asarray(sizes, jnp.int32))

    sizes = jnp.where(number % 4 == 0, named(packed, number // 4), named(usual, number - number // 4 - 1))
    mixed = jax.random.permutation(jax.random.fold_in(own, 3), count)
    donor, taker = mixed[0:count // 2 * 2:2], mixed[1:count // 2 * 2:2]
    slack = jnp.minimum(sizes[donor] - 1, bound - sizes[taker]) // 2
    slack = jnp.where((donor == ranking[0]) | (taker == ranking[0]) | (sizes[taker] == 0), 0, jnp.maximum(slack, 0))
    passed = jax.random.randint(jax.random.fold_in(own, 4), (count // 2,), 0, 1 << 20) % (slack + 1)
    sizes = sizes.at[donor].add(-passed).at[taker].add(passed)
    members = jnp.searchsorted(jnp.cumsum(sizes), jnp.arange(rows * top), side="right").astype(jnp.int32)
    grid = members.reshape(top, rows).T
    grid = grid[jax.random.permutation(jax.random.fold_in(own, 1), rows)]
    offset_by = jax.random.randint(jax.random.fold_in(own, 2), (rows, 1), 0, top)
    return jnp.take_along_axis(grid, (jnp.arange(top)[None, :] + offset_by) % top, axis=1)


def shares(amount, total, bound, skew, full):
    loads = [(1 << 20) // math.isqrt(standing ** skew) + 1 for standing in range(1, amount + 1)]
    largest = bound if full else min(bound, max(-(-total // amount), total * loads[0] // sum(loads)))
    least = 1 if total - largest >= amount - 1 else 0
    given, surplus = [largest] + [least] * (amount - 1), total - largest - least * (amount - 1)
    while surplus > 0:
        free = [i for i in range(1, amount) if given[i] < largest] or [i for i in range(1, amount) if given[i] < bound]
        mass, remaining = sum([loads[i] for i in free]), surplus
        for i in free:
            more = min(bound - given[i], max(1, remaining * loads[i] // mass), surplus)
            given[i] = given[i] + more
            surplus = surplus - more
    return np.array(given)


def normal_values(rng, extent, width, limit, shards=(), kind=jnp.bfloat16):
    array = jax.random.normal(rng, extent, jnp.float32) * width
    if len(shards) > 0:
        array = level_of(rng, extent, shards, -0.22, 0.18) * array
    return jnp.clip(array, min=-limit, max=limit).astype(kind)


def setup_inputs(seed: int = 0) -> dict:
    key_of = jax.random.split(jax.random.key(seed), 22)
    tokens = normal_values(key_of[0], (TOKENS, D), 1.0, 6.0, ((0, 8),))
    norm_attn = jnp.clip(1.0 + 0.1 * jax.random.normal(key_of[1], (D,), jnp.float32), 0.5, 1.5).astype(jnp.bfloat16)
    w_query = normal_values(key_of[2], (D, HQ), D ** -0.5, 0.125, ((0, 8), (1, 4)))
    b_query = normal_values(key_of[3], (HQ,), 0.5, 3.0)
    w_key = normal_values(key_of[4], (D, HQ), D ** -0.5, 0.125, ((0, 8), (1, 4)))
    b_key = normal_values(key_of[5], (HQ,), 0.5, 3.0)
    w_value = normal_values(key_of[6], (D, HQ), D ** -0.5, 0.125, ((0, 8), (1, 4)))
    b_value = normal_values(key_of[7], (HQ,), 0.5, 3.0)
    w_output = normal_values(key_of[8], (HQ, D), (HQ // 64) ** -0.5, 1.0, ((0, 4), (1, 8)))
    norm_ffn = jnp.clip(1.0 + 0.1 * jax.random.normal(key_of[9], (D,), jnp.float32), 0.5, 1.5).astype(jnp.bfloat16)
    w_router = normal_values(key_of[10], (D, EXPERTS), (4 * D) ** -0.5, 0.0625)
    shared_mix = normal_values(key_of[11], (D,), D ** -0.5, 0.125)
    shared_gate = normal_values(key_of[12], (D, SH), D ** -0.5, 0.125, ((0, 8), (1, 4)))
    shared_up = normal_values(key_of[13], (D, SH), D ** -0.5, 0.125, ((0, 8), (1, 4)))
    shared_down = normal_values(key_of[14], (SH, D), (SH // 4) ** -0.5, 0.15625, ((0, 4), (1, 8)))
    expert_gate = normal_values(key_of[15], (EXPERTS, D, FFE), D ** -0.5, 0.125, ((0, 8), (2, 4)))
    expert_up = normal_values(key_of[16], (EXPERTS, D, FFE), D ** -0.5, 0.125, ((0, 8), (2, 4)))
    expert_down = normal_values(key_of[17], (EXPERTS, FFE, D), (max(FFE // 64, 1)) ** -0.5, 1.25, ((0, 8), (1, 4)))
    routes_keys = jax.random.split(jax.random.fold_in(key_of[18], 1), TOKENS // TOK_DEV)
    routes_turns = jax.random.permutation(jax.random.fold_in(key_of[18], 3), TOKENS // TOK_DEV)
    routes = jax.vmap(lambda own, number: shared_out(jax.random.fold_in(key_of[18], 2), own, number, TOK_DEV, EXPERTS, TOP, CAP, 1))(routes_keys, routes_turns).reshape((TOKENS, TOP))
    seq_lengths = draw_seq_lengths(jax.random.fold_in(key_of[21], 71), 0)
    cotangent = normal_values(key_of[20], (TOKENS, D), 1.0, 6.0, ((0, 8),))
    return {"tokens": tokens, "norm_attn": norm_attn, "w_query": w_query, "b_query": b_query, "w_key": w_key, "b_key": b_key, "w_value": w_value, "b_value": b_value, "w_output": w_output, "norm_ffn": norm_ffn, "w_router": w_router, "shared_mix": shared_mix, "shared_gate": shared_gate, "shared_up": shared_up, "shared_down": shared_down, "expert_gate": expert_gate, "expert_up": expert_up, "expert_down": expert_down, "routes": routes, "seq_lengths": seq_lengths, "cotangent": cotangent}


epsilon = 1e-06
rope_base = 1000000.0

@jax.custom_vjp
def low(v):
    return lax.optimization_barrier(v.astype(jnp.bfloat16)).astype(jnp.float32)

@jax.custom_vjp
def low_back(v):
    return v

def low_keep(v):
    return (low(v), None)

def low_pass(kept, grad):
    return (grad,)

def back_keep(v):
    return (v, None)

def back_low(kept, grad):
    return (low(grad),)
low.defvjp(low_keep, low_pass)
low_back.defvjp(back_keep, back_low)

def highest(left, right):
    return jnp.dot(left, right, precision=lax.Precision.HIGHEST)

def rms_norm(values_in, scaling):
    return values_in * lax.rsqrt(lax.optimization_barrier(jnp.mean(values_in * values_in, axis=-1, keepdims=True)) + epsilon) * scaling

def rotate_half(values_in):
    half_size = values_in.shape[-1] // 2
    return jnp.concatenate([-values_in[..., half_size:], values_in[..., :half_size]], axis=-1)

def rope_tables(positions):
    exponent = jnp.arange(0, HD, 2, dtype=jnp.float32) / HD
    frequency = rope_base ** (-exponent)
    angles = positions.astype(jnp.float32)[:, None] * frequency[None, :]
    angles = jnp.concatenate([angles, angles], axis=-1)
    return (jnp.cos(angles)[:, None, :], jnp.sin(angles)[:, None, :])

def seq_layout(lengths, length_total):
    seq_ends = jnp.cumsum(lengths).astype(jnp.int32)
    starts = (seq_ends - lengths).astype(jnp.int32)
    places = jnp.arange(length_total, dtype=jnp.int32)
    member = (places[:, None] >= starts[None, :]) & (places[:, None] < seq_ends[None, :])
    seq_id = lax.optimization_barrier(jnp.sum((places[:, None] >= seq_ends[None, :]).astype(jnp.int32), axis=1)).astype(jnp.int32)
    offset = lax.optimization_barrier(jnp.sum(jnp.where(member, starts[None, :], 0), axis=1)).astype(jnp.int32)
    return (seq_id, places - offset)

def slot_table(routes):
    per_device = routes.reshape(DEVICES, TOK_DEV * TOP)
    hits = (per_device[:, :, None] == jnp.arange(EXPERTS, dtype=jnp.int32)[None, None, :]).astype(jnp.int32)
    slots = lax.optimization_barrier(jnp.sum((jnp.cumsum(hits, axis=1) - 1) * hits, axis=2)).astype(jnp.int32)
    device_ids = jnp.arange(DEVICES, dtype=jnp.int32)[:, None]
    place_at = ((per_device * DEVICES + device_ids) * CAP + slots).reshape(-1).astype(jnp.int32)
    table = jnp.full((EXPERTS * DEVICES * CAP,), TOKENS * TOP, jnp.int32)
    table = table.at[place_at].set(jnp.arange(TOKENS * TOP, dtype=jnp.int32))
    return (place_at, table.reshape(EXPERTS, DEVICES * CAP))

def attend_block(blocks):
    query, keys, values_in, seq_id, positions = blocks
    raw = low_back(jnp.einsum('qhd,khd->hqk', query, keys, precision=lax.Precision.HIGHEST)) * HD ** (-0.5)
    allowed = (seq_id[:, None] == seq_id[None, :]) & (positions[None, :] <= positions[:, None])
    masked = jnp.where(allowed[None], raw, -1e+30)
    probs = jax.nn.softmax(masked, axis=-1)
    return jnp.einsum('hqk,khd->qhd', low(probs), values_in, precision=lax.Precision.HIGHEST)

def forward(tokens, norm_attn, w_query, b_query, w_key, b_key, w_value, b_value, w_output, norm_ffn, w_router, shared_mix, shared_gate, shared_up, shared_down, expert_gate, expert_up, expert_down, layout):
    seq_id, positions, choose, place_at, table = layout
    h_one = low(rms_norm(tokens, norm_attn))
    query_pre = low_back(highest(h_one, w_query) + b_query)
    key_pre = low_back(highest(h_one, w_key) + b_key)
    value_in = low(low_back(highest(h_one, w_value) + b_value))
    cosine, sine = rope_tables(positions)
    query_pre = query_pre.reshape(TOKENS, HEADS, HD)
    key_pre = key_pre.reshape(TOKENS, HEADS, HD)
    query_rot = low(query_pre * cosine + rotate_half(query_pre) * sine)
    key_rot = low(key_pre * cosine + rotate_half(key_pre) * sine)
    blocks = (query_rot.reshape(DEVICES, TOK_DEV, HEADS, HD), key_rot.reshape(DEVICES, TOK_DEV, HEADS, HD), value_in.reshape(DEVICES, TOK_DEV, HEADS, HD), seq_id.reshape(DEVICES, TOK_DEV), positions.reshape(DEVICES, TOK_DEV))
    attended = lax.map(jax.checkpoint(attend_block), blocks)
    attended = low(low_back(attended.reshape(TOKENS, HQ)))
    x_two = tokens + low_back(highest(attended, w_output))
    h_two = low(rms_norm(x_two, norm_ffn))
    router_probs = jax.nn.softmax(highest(h_two, w_router), axis=-1)
    gates = lax.optimization_barrier(jnp.sum(choose * router_probs[:, None, :], axis=-1))
    gate_shared = low_back(highest(h_two, shared_gate))
    up_shared = low_back(highest(h_two, shared_up))
    hidden_shared = low(jax.nn.silu(gate_shared) * up_shared)
    out_shared = low_back(highest(hidden_shared, shared_down))
    mix_gate = jax.nn.sigmoid(highest(h_two, shared_mix))
    h_padded = jnp.concatenate([h_two, jnp.zeros((1, D), jnp.float32)], axis=0)

    def one_expert(pieces):
        gate_w, up_w, down_w, index_row = pieces
        inputs = low_back(h_padded[index_row // TOP])
        gate_e = low_back(highest(inputs, gate_w))
        up_e = low_back(highest(inputs, up_w))
        hidden_e = low(jax.nn.silu(gate_e) * up_e)
        return low(low_back(highest(hidden_e, down_w)))
    expert_rows = lax.map(jax.checkpoint(one_expert), (expert_gate, expert_up, expert_down, table))
    picked = expert_rows.reshape(-1, D)[place_at].reshape(TOKENS, TOP, D)
    routed = lax.optimization_barrier(jnp.sum(gates[:, :, None] * picked, axis=1))
    return x_two + routed + mix_gate[:, None] * out_shared

def reference(tokens, norm_attn, w_query, b_query, w_key, b_key, w_value, b_value, w_output, norm_ffn, w_router, shared_mix, shared_gate, shared_up, shared_down, expert_gate, expert_up, expert_down, routes, seq_lengths, cotangent):
    seq_id, positions = jax.vmap(lambda lengths: seq_layout(lengths, TOK_DEV))(seq_lengths)
    seq_id = seq_id.reshape(-1)
    positions = positions.reshape(-1)
    choose = (routes[:, :, None] == jnp.arange(EXPERTS, dtype=jnp.int32)[None, None, :]).astype(jnp.float32)
    place_at, table = slot_table(routes)
    layout = (seq_id, positions, choose, place_at, table)
    floats = (tokens.astype(jnp.float32), norm_attn.astype(jnp.float32), w_query.astype(jnp.float32), b_query.astype(jnp.float32), w_key.astype(jnp.float32), b_key.astype(jnp.float32), w_value.astype(jnp.float32), b_value.astype(jnp.float32), w_output.astype(jnp.float32), norm_ffn.astype(jnp.float32), w_router.astype(jnp.float32), shared_mix.astype(jnp.float32), shared_gate.astype(jnp.float32), shared_up.astype(jnp.float32), shared_down.astype(jnp.float32), expert_gate.astype(jnp.float32), expert_up.astype(jnp.float32), expert_down.astype(jnp.float32))

    def wrapped(*params):
        return forward(*params, layout)
    block_out, pullback = jax.vjp(wrapped, *floats)
    grads = pullback(cotangent.astype(jnp.float32))
    return (block_out.astype(jnp.bfloat16), grads[0], grads[1], grads[2], grads[3], grads[4], grads[5], grads[6], grads[7], grads[8], grads[9], grads[10], grads[11], grads[12], grads[13], grads[14], grads[15], grads[16], grads[17])
```

```python
import jax
import jax.numpy as jnp
from jax import lax
from jax.sharding import PartitionSpec as P

HD = 128
TOP = 4

epsilon = 1e-06
rope_base = 1000000.0

RING, PAIR, SHARD = "ring", "pair", "shard"

BF, F32 = jnp.bfloat16, jnp.float32


def rotate_half(values_in):
    half_size = values_in.shape[-1] // 2
    return jnp.concatenate([-values_in[..., half_size:], values_in[..., :half_size]], axis=-1)


def rope_tables(positions, head_size):
    exponent = jnp.arange(0, head_size, 2, dtype=F32) / head_size
    frequency = rope_base ** (-exponent)
    angles = positions.astype(F32)[..., None] * frequency
    angles = jnp.concatenate([angles, angles], axis=-1)
    return (jnp.cos(angles), jnp.sin(angles))


def seq_layout(lengths, length_total):
    seq_ends = jnp.cumsum(lengths)
    starts = seq_ends - lengths
    places = jnp.arange(length_total, dtype=jnp.int32)
    member = (places[:, None] >= starts[None, :]) & (places[:, None] < seq_ends[None, :])
    seq_id = jnp.sum((places[:, None] >= seq_ends[None, :]).astype(jnp.int32), axis=1)
    offset = jnp.sum(jnp.where(member, starts[None, :], 0), axis=1)
    return (seq_id, places - offset)


def silu_slope(values_in):
    logistic = jax.nn.sigmoid(values_in)
    return logistic * (1.0 + values_in * (1.0 - logistic))


def norm_back(grad_normed, values_in, inverse, gain_wide, upstream_rows):
    normed = grad_normed * gain_wide
    return (
        upstream_rows
        + inverse * normed
        - values_in * inverse**3 * jnp.mean(normed * values_in, axis=1, keepdims=True)
    )


def dot(left, right, contract):
    return lax.dot_general(
        left, right, (((contract[0],), (contract[1],)), ((), ())), preferred_element_type=F32
    )


def two_parts(values_in):
    high = values_in.astype(BF)
    return high, (values_in - high.astype(F32)).astype(BF)


def flip(values_in, axis, bit):
    size = lax.axis_size(axis)
    return lax.ppermute(values_in, axis, [(i, i ^ bit) for i in range(size)])


def shift(values_in, step):
    size = lax.axis_size(RING)
    return lax.ppermute(values_in, RING, [(i, (i + step) % size) for i in range(size)])


def shard_bits():
    bits, bit = [], lax.axis_size(SHARD) // 2
    while bit:
        bits.append(bit)
        bit //= 2
    return bits


def team_bits():
    return [(PAIR, 1)] + [(SHARD, bit) for bit in shard_bits()]


def team_order():
    order = [(0, 0)]
    for axis, bit in team_bits():
        order += [(p ^ bit, s) if axis == PAIR else (p, s ^ bit) for p, s in order]
    return order


def team_sum(values_in):
    for axis, bit in reversed(team_bits()):
        half = values_in.shape[0] // 2
        got = flip(values_in[half:].astype(BF), axis, bit)
        values_in = values_in[:half].astype(F32) + got.astype(F32)
    return values_in


def shard_sum(values_in):
    for bit in reversed(shard_bits()):
        half = values_in.shape[0] // 2
        got = flip(values_in[half:].astype(BF), SHARD, bit)
        values_in = values_in[:half].astype(F32) + got.astype(F32)
    return values_in


def ring_gather(block):
    size = lax.axis_size(RING)
    ups, downs = [block], []
    for _ in range(size // 2):
        ups.append(shift(ups[-1], 1))
    last = block
    for _ in range((size - 1) // 2):
        last = shift(last, -1)
        downs.append(last)
    return ups + downs


def ring_sum(blocks):
    size = lax.axis_size(RING)
    back = size // 2
    total = blocks[0].astype(F32)
    running = blocks[back] if back else None
    for k in range(back, 0, -1):
        got = shift(running.astype(BF), -1).astype(F32)
        if k > 1:
            running = got + blocks[k - 1].astype(F32)
        else:
            total = total + got
    ahead = (size - 1) // 2
    running = blocks[back + ahead] if ahead else None
    for k in range(ahead, 0, -1):
        got = shift(running.astype(BF), 1).astype(F32)
        if k > 1:
            running = got + blocks[back + k - 1].astype(F32)
        else:
            total = total + got
    return total


def expert_gather(block):
    return [(b, flip(b, PAIR, 1)) for b in ring_gather(block)]


def expert_sum(pairs):
    return ring_sum(
        [own.astype(F32) + flip(other.astype(BF), PAIR, 1).astype(F32) for own, other in pairs]
    )


def all_sum(values_in):
    for axis in (SHARD, PAIR, RING):
        bit = 1
        while bit < lax.axis_size(axis):
            values_in = values_in + flip(values_in, axis, bit)
            bit *= 2
    return values_in


def local(
    tokens,
    norm_attn,
    w_query,
    b_query,
    w_key,
    b_key,
    w_value,
    b_value,
    w_output,
    norm_ffn,
    w_router,
    shared_mix,
    shared_gate,
    shared_up,
    shared_down,
    expert_gate,
    expert_up,
    expert_down,
    routes,
    seq_lengths,
    cotangent,
):
    n_shard = lax.axis_size(SHARD)
    ring_at, pair_at, shard_at = (lax.axis_index(a) for a in (RING, PAIR, SHARD))
    expert_at = ring_at * 2 + pair_at
    group_rows, model_width = tokens.shape
    rows = group_rows // n_shard
    experts = w_router.shape[1]
    capacity = rows * TOP * 5 // (4 * experts)
    slot_rows = experts * capacity
    scale = HD ** (-0.5)
    order = team_order()

    def block_of(values_in, flipped):
        return lax.dynamic_slice_in_dim(values_in, (shard_at ^ flipped) * rows, rows, 0)

    def team_rows(values_in):
        near = {s: block_of(values_in, s) for p, s in order if p == 0}
        far = [flip(near[0], PAIR, 1)]
        for bit in shard_bits():
            got = flip(jnp.concatenate(far, axis=0), SHARD, bit)
            far += [got[i * rows : (i + 1) * rows] for i in range(len(far))]
        far = dict(zip([s for p, s in order if p == 1], far, strict=True))
        return near, far, jnp.concatenate([far[s] if p else near[s] for p, s in order], axis=0)

    def halves(values_in):
        return values_in.reshape(2, values_in.shape[0] // 2, values_in.shape[1])

    def gather_units(parts):
        pack = jnp.concatenate([halves(part) for part in parts], axis=1)
        mine = lax.dynamic_index_in_dim(pack, pair_at, 0, keepdims=False)
        theirs = lax.dynamic_index_in_dim(pack, 1 - pair_at, 0, keepdims=False)
        got = flip(theirs, PAIR, 1)
        block = jnp.where(
            pair_at == 0,
            jnp.concatenate([mine, got], axis=1),
            jnp.concatenate([got, mine], axis=1),
        )
        return lax.all_gather(block, RING, axis=1, tiled=True)

    def scatter_units(grads):
        summed = lax.psum_scatter(
            jnp.concatenate([g.astype(BF) for g in grads], axis=0),
            RING,
            scatter_dimension=1,
            tiled=True,
        )
        width = summed.shape[1] // 2
        mine = lax.dynamic_slice_in_dim(summed, pair_at * width, width, 1)
        theirs = lax.dynamic_slice_in_dim(summed, (1 - pair_at) * width, width, 1)
        got = flip(theirs, PAIR, 1)
        first, second = jnp.where(pair_at == 0, mine, got), jnp.where(pair_at == 0, got, mine)
        out, at = [], 0
        for g in grads:
            n = g.shape[0]
            out.append(jnp.concatenate([first[at : at + n], second[at : at + n]], axis=0).astype(F32))
            at += n
        return out

    attn_w = gather_units([w_query.T, w_key.T, w_value.T, w_output])
    width_here = attn_w.shape[0] // 4
    heads_here = width_here // HD
    qkv_w, output_w = attn_w[: 3 * width_here], attn_w[3 * width_here :]
    shared_w = gather_units([shared_gate.T, shared_up.T, shared_down])
    units_here = shared_w.shape[0] // 3
    shared_gate_w, shared_up_w, shared_down_w = (
        shared_w[i * units_here : (i + 1) * units_here] for i in range(3)
    )
    expert_pack = [jnp.concatenate([expert_gate[0].T, expert_up[0].T, expert_down[0]], axis=0)]
    for bit in shard_bits():
        expert_pack = expert_pack + [flip(part, SHARD, bit) for part in expert_pack]
    piece = expert_down.shape[1]
    gate_w, up_w, down_w = (
        jnp.concatenate([part[i * piece : (i + 1) * piece] for part in expert_pack], axis=0)
        for i in range(3)
    )

    routes_in = jnp.concatenate([b for pair in expert_gather(routes.T) for b in pair], axis=1)
    chosen = jnp.any(routes_in == expert_at, axis=0)
    hits = chosen.astype(jnp.int32)
    places = jnp.arange(hits.shape[0], dtype=jnp.int32)
    slot = jnp.sum(jnp.where(places[None, :] < places[:, None], hits[None, :], 0), axis=1)
    slot_ids = jnp.arange(slot_rows, dtype=jnp.int32)
    table = jnp.sum(
        jnp.where((slot[None, :] == slot_ids[:, None]) & chosen[None, :], places[None, :], 0), axis=1
    )
    filled = slot_ids < jnp.sum(hits)

    def returned(values_in):
        taken = jnp.where(chosen[:, None], jnp.take(values_in, slot, axis=0, mode="clip"), jnp.zeros((), BF))
        blocks = [taken[i * rows : (i + 1) * rows] for i in range(experts)]
        return [(blocks[2 * i], blocks[2 * i + 1]) for i in range(experts // 2)]

    tokens_near, _, tokens_team = team_rows(tokens)
    far_lengths = flip(seq_lengths, PAIR, 1)
    lengths = jnp.stack(
        [
            lax.dynamic_index_in_dim(far_lengths if p else seq_lengths, shard_at ^ s, 0, False)
            for p, s in order
        ]
    )
    seq_id, positions = jax.vmap(lambda row: seq_layout(row, rows))(lengths)
    cosine, sine = rope_tables(positions, HD)
    cosine, sine = cosine[:, :, None, :], sine[:, :, None, :]
    allowed = (seq_id[:, :, None] == seq_id[:, None, :]) & (
        positions[:, None, :] <= positions[:, :, None]
    )
    resid_team = tokens_team.astype(F32)
    gain_one = norm_attn.astype(F32)
    inv_one_team = lax.rsqrt(jnp.mean(resid_team * resid_team, axis=1, keepdims=True) + epsilon)
    h_one = (resid_team * inv_one_team * gain_one).astype(BF)
    head_start = (shard_at * 2 + pair_at) * width_here
    qkv_b = jnp.concatenate(
        [lax.dynamic_slice_in_dim(b, head_start, width_here, 0) for b in (b_query, b_key, b_value)]
    ).astype(F32)
    qkv = dot(h_one, qkv_w, (1, 1)) + qkv_b
    team = len(order)

    def heads(values_in):
        return values_in.reshape(team, rows, heads_here, HD)

    query_pre, key_pre, value_pre = (
        heads(qkv[:, i * width_here : (i + 1) * width_here]) for i in range(3)
    )
    query_rot = (query_pre * cosine + rotate_half(query_pre) * sine).astype(BF)
    key_rot = (key_pre * cosine + rotate_half(key_pre) * sine).astype(BF)
    value_low = value_pre.astype(BF)
    raw_scores = (
        jnp.einsum("bqhd,bkhd->bhqk", query_rot, key_rot, preferred_element_type=F32) * scale
    )
    masked = jnp.where(allowed[:, None], raw_scores, -1e30)
    probs = jax.nn.softmax(masked, axis=-1)
    probs_low = probs.astype(BF)
    attended = jnp.einsum("bhqk,bkhd->bqhd", probs_low, value_low, preferred_element_type=F32)
    attended_low = attended.reshape(team * rows, width_here).astype(BF)
    attn_out = team_sum(dot(attended_low, output_w, (1, 0)))

    resid_in = tokens_near[0].astype(F32)
    x_two = resid_in + attn_out
    gain_two = norm_ffn.astype(F32)
    inv_two = lax.rsqrt(jnp.mean(x_two * x_two, axis=1, keepdims=True) + epsilon)
    h_two = (x_two * inv_two * gain_two).astype(BF)

    h_routed = expert_gather(h_two)
    h_list = list(h_routed[0])
    for bit in shard_bits():
        got = flip(jnp.concatenate(h_list, axis=0), SHARD, bit)
        h_list += [got[i * rows : (i + 1) * rows] for i in range(len(h_list))]
    h_team = jnp.concatenate(h_list, axis=0)
    rows_in = jnp.concatenate([b for pair in h_routed for b in pair], axis=0)
    rows_in = jnp.take(rows_in, table, axis=0, mode="clip")

    up_near, up_far, up_team = team_rows(cotangent)
    upstream = up_near[0].astype(F32)
    up_ring = ring_gather(up_near[0])
    up_routed = [up_near[0], up_far[0]] + [
        b for block in up_ring[1:] for b in (block, flip(block, PAIR, 1))
    ]
    up_rows = jnp.take(jnp.concatenate(up_routed, axis=0), table, axis=0, mode="clip")

    row_probs = jax.nn.softmax(
        jnp.dot(rows_in, w_router, preferred_element_type=F32), axis=-1
    )
    own_expert = (jnp.arange(experts, dtype=jnp.int32) == expert_at).astype(F32)
    row_gate = jnp.sum(row_probs * own_expert, axis=1) * filled.astype(F32)
    gate_e = dot(rows_in, gate_w, (1, 1))
    up_e = dot(rows_in, up_w, (1, 1))
    hidden_e = (jax.nn.silu(gate_e) * up_e).astype(BF)
    grad_rows = (row_gate[:, None] * up_rows.astype(F32)).astype(BF)
    grad_hidden_e = dot(grad_rows, down_w, (1, 1))
    grad_gate_e = (grad_hidden_e * up_e * silu_slope(gate_e)).astype(BF)
    grad_up_e = (grad_hidden_e * jax.nn.silu(gate_e)).astype(BF)
    gate_share = jnp.sum(hidden_e.astype(F32) * grad_hidden_e, axis=1)
    grad_logit = gate_share[:, None] * (own_expert - row_probs)
    logit_parts = jnp.concatenate(two_parts(grad_logit), axis=1)
    router_twice = jnp.concatenate([w_router, w_router], axis=1)
    grad_inputs = (
        dot(grad_gate_e, gate_w, (1, 0))
        + dot(grad_up_e, up_w, (1, 0))
        + dot(logit_parts, router_twice, (1, 1))
    ).astype(BF)
    grad_router = dot(logit_parts, rows_in, (0, 0))
    grad_router = grad_router[:experts] + grad_router[experts:]

    mix_team = jax.nn.sigmoid(jnp.dot(h_team, shared_mix, preferred_element_type=F32))
    gate_s = dot(h_team, shared_gate_w, (1, 1))
    up_s = dot(h_team, shared_up_w, (1, 1))
    hidden_s = (jax.nn.silu(gate_s) * up_s).astype(BF)
    grad_out_s = (mix_team[:, None] * up_team.astype(F32)).astype(BF)
    grad_hidden_s = dot(grad_out_s, shared_down_w, (1, 1))
    grad_gate_s = (grad_hidden_s * up_s * silu_slope(gate_s)).astype(BF)
    grad_up_s = (grad_hidden_s * jax.nn.silu(gate_s)).astype(BF)
    grad_mix = jnp.sum(hidden_s.astype(F32) * grad_hidden_s, axis=1) * (1.0 - mix_team)
    grad_h_shared = shard_sum(
        dot(grad_gate_s, shared_gate_w, (1, 0))
        + dot(grad_up_s, shared_up_w, (1, 0))
        + grad_mix[:, None] * shared_mix.astype(F32)[None, :]
    )
    mix_parts = jnp.stack(two_parts(grad_mix), axis=1)
    grad_mix_w = jnp.sum(dot(mix_parts, h_team, (0, 0)), axis=0)

    def with_shared(pairs, shared_rows):
        own, other = pairs[0]
        first = (own.astype(F32) + shared_rows[:rows], other.astype(F32) + shared_rows[rows:])
        return [first] + pairs[1:]

    grad_h_two = expert_sum(with_shared(returned(grad_inputs), grad_h_shared))
    grad_x_two = norm_back(grad_h_two, x_two, inv_two, gain_two, upstream)
    grad_norm_ffn = jnp.sum(grad_h_two * x_two * inv_two, axis=0)

    out_e = dot(hidden_e, down_w, (1, 0)).astype(BF)
    out_e = (row_gate[:, None] * out_e.astype(F32)).astype(BF)
    out_s = shard_sum(mix_team[:, None] * dot(hidden_s, shared_down_w, (1, 0)))
    block_out = (x_two + expert_sum(with_shared(returned(out_e), out_s))).astype(BF)

    grad_shared_gate, grad_shared_up, grad_shared_down = scatter_units(
        [
            dot(grad_gate_s, h_team, (0, 0)),
            dot(grad_up_s, h_team, (0, 0)),
            dot(hidden_s, grad_out_s, (0, 0)),
        ]
    )

    def expert_scatter(units, across):
        half = units.shape[1] // 2
        kept = dot(units[:, :half], across, (0, 0))
        given = dot(units[:, half:], across, (0, 0))
        for bit in reversed(shard_bits()):
            kept = kept + flip(given.astype(BF), SHARD, bit).astype(F32)
            half = kept.shape[0] // 2
            kept, given = kept[:half], kept[half:]
        return jnp.concatenate([kept, given], axis=0)

    grad_expert_gate = expert_scatter(grad_gate_e, rows_in)
    grad_expert_up = expert_scatter(grad_up_e, rows_in)
    grad_expert_down = expert_scatter(hidden_e, grad_rows)

    grad_attn = grad_x_two.astype(BF)
    for axis, bit in team_bits():
        grad_attn = jnp.concatenate([grad_attn, flip(grad_attn, axis, bit)], axis=0)
    grad_attended = heads(dot(grad_attn, output_w, (1, 1)).astype(BF))
    grad_probs = jnp.einsum("bqhd,bkhd->bhqk", grad_attended, value_low, preferred_element_type=F32)
    grad_value = jnp.einsum(
        "bhqk,bqhd->bkhd", probs_low, grad_attended, preferred_element_type=F32
    ).astype(BF)
    row_delta = jnp.sum(probs * grad_probs, axis=-1, keepdims=True)
    grad_scores = (probs * (grad_probs - row_delta) * scale).astype(BF)
    grad_query = jnp.einsum("bhqk,bkhd->bqhd", grad_scores, key_rot, preferred_element_type=F32)
    grad_key = jnp.einsum("bhqk,bqhd->bkhd", grad_scores, query_rot, preferred_element_type=F32)
    grad_query = (grad_query * cosine - rotate_half(grad_query * sine)).astype(BF)
    grad_key = (grad_key * cosine - rotate_half(grad_key * sine)).astype(BF)
    grad_qkv = jnp.concatenate(
        [g.reshape(team * rows, width_here) for g in (grad_query, grad_key, grad_value)], axis=1
    )
    grad_h_one = team_sum(dot(grad_qkv, qkv_w, (1, 0)))
    grad_qkv_w = dot(grad_qkv, h_one, (0, 0))
    grad_query_w, grad_key_w, grad_value_w, grad_output_w = scatter_units(
        [grad_qkv_w[i * width_here : (i + 1) * width_here] for i in range(3)]
        + [dot(attended_low, grad_attn, (0, 0))]
    )
    grad_qkv_b = jnp.sum(grad_qkv.astype(F32), axis=0).reshape(3, width_here)
    grad_qkv_b = lax.dynamic_update_slice_in_dim(
        jnp.zeros((3, b_query.shape[0]), F32), grad_qkv_b, head_start, 1
    )
    inv_one = lax.rsqrt(jnp.mean(resid_in * resid_in, axis=1, keepdims=True) + epsilon)
    grad_norm_attn = jnp.sum(grad_h_one * resid_in * inv_one, axis=0)
    grad_tokens = norm_back(grad_h_one, resid_in, inv_one, gain_one, grad_x_two)

    small = all_sum(
        jnp.concatenate(
            [
                grad_qkv_b,
                jnp.stack([grad_norm_attn, grad_norm_ffn, grad_mix_w]),
                grad_router,
            ],
            axis=0,
        )
    )
    return (
        block_out,
        grad_tokens,
        small[3],
        grad_query_w.T,
        small[0],
        grad_key_w.T,
        small[1],
        grad_value_w.T,
        small[2],
        grad_output_w,
        small[4],
        small[6:].T,
        small[5],
        grad_shared_gate.T,
        grad_shared_up.T,
        grad_shared_down,
        grad_expert_gate.T[None],
        grad_expert_up.T[None],
        grad_expert_down[None],
    )


def solution(mesh):
    experts, shards = mesh.shape["expert"], mesh.shape["shard"]
    grid = jax.sharding.Mesh(
        mesh.devices.reshape(experts // 2, 2, shards), (RING, PAIR, SHARD)
    )
    expert = (RING, PAIR)
    every = (RING, PAIR, SHARD)
    return jax.shard_map(
        local,
        mesh=grid,
        in_specs=(
            P(expert, None),
            P(),
            P(expert, SHARD),
            P(),
            P(expert, SHARD),
            P(),
            P(expert, SHARD),
            P(),
            P(SHARD, expert),
            P(),
            P(),
            P(),
            P(expert, SHARD),
            P(expert, SHARD),
            P(SHARD, expert),
            P(expert, None, SHARD),
            P(expert, None, SHARD),
            P(expert, SHARD, None),
            P(every, None),
            P(expert, None),
            P(expert, None),
        ),
        out_specs=(
            P(every, None),
            P(every, None),
            P(),
            P(expert, SHARD),
            P(),
            P(expert, SHARD),
            P(),
            P(expert, SHARD),
            P(),
            P(SHARD, expert),
            P(),
            P(),
            P(),
            P(expert, SHARD),
            P(expert, SHARD),
            P(SHARD, expert),
            P(expert, None, SHARD),
            P(expert, None, SHARD),
            P(expert, SHARD, None),
        ),
        check_vma=False,
    )
```

```python
import functools

import jax
import jax.numpy as jnp
from jax import lax
from jax.experimental import pallas as pl
from jax.experimental.pallas import tpu as pltpu
from jax.sharding import PartitionSpec as P

HD = 128
TOP = 4
LANES = 128

NO_COST = pl.CostEstimate(flops=0, bytes_accessed=0, transcendentals=0)

epsilon = 1e-06
rope_base = 1000000.0

RING, PAIR, SHARD = "ring", "pair", "shard"

BF, F32 = jnp.bfloat16, jnp.float32

ATTN_STEPS, ATTN_BACK_STEPS = 4, 2


def rope_tables(positions, head_size):
    exponent = jnp.arange(0, head_size, 2, dtype=F32) / head_size
    frequency = rope_base ** (-exponent)
    angles = positions.astype(F32)[..., None] * frequency
    cosine, sine = jnp.cos(angles), jnp.sin(angles)
    return (
        jnp.concatenate([cosine, cosine], axis=-1),
        jnp.concatenate([-sine, sine], axis=-1),
    )


def seq_positions(lengths, length_total):
    seq_ends = jnp.cumsum(lengths)
    starts = seq_ends - lengths
    places = jnp.arange(length_total, dtype=jnp.int32)
    member = (places[:, None] >= starts[None, :]) & (places[:, None] < seq_ends[None, :])
    return places - jnp.sum(jnp.where(member, starts[None, :], 0), axis=1)


def norm_back(grad_normed, values_in, inverse, gain_wide, upstream_rows):
    normed = grad_normed * gain_wide
    return (
        upstream_rows
        + inverse * normed
        - values_in * inverse**3 * jnp.mean(normed * values_in, axis=1, keepdims=True)
    )


def dot(left, right, contract):
    return lax.dot_general(
        left, right, (((contract[0],), (contract[1],)), ((), ())), preferred_element_type=F32
    )


def two_parts(values_in):
    high = values_in.astype(BF)
    return high, (values_in - high.astype(F32)).astype(BF)


def swap_halves(values_in):
    return pltpu.roll(values_in, HD // 2, 1)


def causal_probs(query, key, start, scale):
    raw = dot(query, key, (1, 1)) * scale
    row = lax.broadcasted_iota(jnp.int32, raw.shape, 0)
    column = lax.broadcasted_iota(jnp.int32, raw.shape, 1)
    masked = jnp.where((column <= row) & (column >= start), raw, -1e30)
    powers = jnp.exp(masked - jnp.max(masked, axis=-1, keepdims=True))
    return powers / jnp.sum(powers, axis=-1, keepdims=True)


def in_halves(kept_ref, given_ref, made):
    steps = pl.num_programs(0)

    @pl.when(pl.program_id(0) < steps // 2)
    def _():
        kept_ref[...] = made

    @pl.when(pl.program_id(0) >= steps // 2)
    def _():
        given_ref[...] = made


def half_blocks(steps, rows_each, width):
    half = steps // 2
    return [
        pl.BlockSpec((rows_each, width), lambda i: (jnp.minimum(i, half - 1), 0)),
        pl.BlockSpec((rows_each, width), lambda i: (jnp.maximum(i - half, 0), 0)),
    ]


def attention_forward_body(
    rows, heads, scale, h_ref, w_ref, bias_ref, cos_ref, sin_ref, start_ref, kept_ref, given_ref, qkv_ref, att_ref
):
    width = heads * HD
    qkv = dot(h_ref[...], w_ref[: 3 * width], (1, 1)) + bias_ref[...]
    for block in range(h_ref.shape[0] // rows):
        here = slice(block * rows, (block + 1) * rows)
        cosine, sine, start = cos_ref[here], sin_ref[here], start_ref[here]
        for head in range(heads):
            at = [slice(i * width + head * HD, i * width + (head + 1) * HD) for i in range(3)]
            query, key, value = (qkv[here, span] for span in at)
            query = (query * cosine + swap_halves(query) * sine).astype(BF)
            key = (key * cosine + swap_halves(key) * sine).astype(BF)
            value = value.astype(BF)
            for span, kept in zip(at, (query, key, value), strict=True):
                qkv_ref[here, span] = kept
            probs = causal_probs(query, key, start, scale).astype(BF)
            att_ref[here, at[0]] = dot(probs, value, (1, 0)).astype(BF)
    in_halves(kept_ref, given_ref, dot(att_ref[...], w_ref[3 * width :], (1, 0)).astype(BF))


def attention_backward_body(
    rows,
    heads,
    scale,
    grad_ref,
    h_ref,
    w_ref,
    qkv_ref,
    att_ref,
    cos_ref,
    sin_ref,
    start_ref,
    kept_ref,
    given_ref,
    pack_ref,
    bias_ref,
    grad_qkv_ref,
    total_ref,
):
    width = heads * HD
    step = pl.program_id(0)
    grad_att = dot(grad_ref[...], w_ref[3 * width :], (1, 1)).astype(BF)
    for block in range(grad_ref.shape[0] // rows):
        here = slice(block * rows, (block + 1) * rows)
        cosine, sine, start = cos_ref[here], sin_ref[here], start_ref[here]
        for head in range(heads):
            at = [slice(i * width + head * HD, i * width + (head + 1) * HD) for i in range(3)]
            query, key, value = (qkv_ref[here, span] for span in at)
            grad_out = grad_att[here, at[0]]
            probs = causal_probs(query, key, start, scale)
            grad_probs = dot(grad_out, value, (1, 1))
            grad_value = dot(probs.astype(BF), grad_out, (0, 0))
            delta = jnp.sum(probs * grad_probs, axis=-1, keepdims=True)
            grad_scores = (probs * (grad_probs - delta) * scale).astype(BF)
            grad_query = dot(grad_scores, key, (1, 0))
            grad_key = dot(grad_scores, query, (0, 0))
            grad_query = grad_query * cosine - swap_halves(grad_query) * sine
            grad_key = grad_key * cosine - swap_halves(grad_key) * sine
            for span, made in zip(at, (grad_query, grad_key, grad_value), strict=True):
                grad_qkv_ref[here, span] = made.astype(BF)
    grad_qkv = grad_qkv_ref[...]
    in_halves(kept_ref, given_ref, dot(grad_qkv, w_ref[: 3 * width], (1, 0)).astype(BF))
    bias_share = jnp.sum(grad_qkv.astype(F32), axis=0, keepdims=True)
    qkv_share = dot(grad_qkv, h_ref[...], (0, 0))
    out_share = dot(att_ref[...], grad_ref[...], (0, 0))

    @pl.when(step == 0)
    def _():
        bias_ref[...] = bias_share
        total_ref[: 3 * width] = qkv_share
        total_ref[3 * width :] = out_share

    @pl.when(step > 0)
    def _():
        bias_ref[...] += bias_share
        total_ref[: 3 * width] += qkv_share
        total_ref[3 * width :] += out_share

    @pl.when(step == pl.num_programs(0) - 1)
    def _():
        pack_ref[...] = total_ref[...].astype(BF)


def anywhere():
    return pl.BlockSpec(memory_space=pl.ANY)


def waiting(body, count):
    def run(*refs):
        body(*refs[count:])

    return run


def once_block(*shape):
    return pl.BlockSpec(shape, lambda *i: (0,) * len(shape), pipeline_mode=pl.Buffered(1))


def step_block(rows_each, *rest):
    return pl.BlockSpec((rows_each,) + rest, lambda i: (i,) + (0,) * len(rest))


def whole_block(*shape):
    return pl.BlockSpec(shape, lambda i: (0,) * len(shape))


def attention_forward(h_one, weights, bias, cosine, sine, start, rows, heads, steps, waits=()):
    total, model = h_one.shape
    each, width = total // steps, heads * HD
    return pl.pallas_call(
        waiting(functools.partial(attention_forward_body, rows, heads, HD ** (-0.5)), len(waits)),
        grid=(steps,),
        in_specs=[anywhere()] * len(waits)
        + [
            step_block(each, model),
            whole_block(4 * width, model),
            whole_block(1, 3 * width),
            step_block(each, HD),
            step_block(each, HD),
            step_block(each, 1),
        ],
        out_specs=half_blocks(steps, each, model) + [step_block(each, 3 * width), step_block(each, width)],
        out_shape=[
            jax.ShapeDtypeStruct((total // 2, model), BF),
            jax.ShapeDtypeStruct((total // 2, model), BF),
            jax.ShapeDtypeStruct((total, 3 * width), BF),
            jax.ShapeDtypeStruct((total, width), BF),
        ],
        compiler_params=pltpu.CompilerParams(vmem_limit_bytes=40 << 20),
        cost_estimate=NO_COST,
    )(*waits, h_one, weights, bias, cosine, sine, start)


def attention_backward(grad, h_one, weights, qkv, att, cosine, sine, start, rows, heads, steps, waits=()):
    total, model = h_one.shape
    each, width = total // steps, heads * HD
    return pl.pallas_call(
        waiting(functools.partial(attention_backward_body, rows, heads, HD ** (-0.5)), len(waits)),
        grid=(steps,),
        in_specs=[anywhere()] * len(waits)
        + [
            step_block(each, model),
            step_block(each, model),
            whole_block(4 * width, model),
            step_block(each, 3 * width),
            step_block(each, width),
            step_block(each, HD),
            step_block(each, HD),
            step_block(each, 1),
        ],
        out_specs=half_blocks(steps, each, model) + [whole_block(4 * width, model), whole_block(1, 3 * width)],
        out_shape=[
            jax.ShapeDtypeStruct((total // 2, model), BF),
            jax.ShapeDtypeStruct((total // 2, model), BF),
            jax.ShapeDtypeStruct((4 * width, model), BF),
            jax.ShapeDtypeStruct((1, 3 * width), F32),
        ],
        scratch_shapes=[
            pltpu.VMEM((each, 3 * width), BF),
            pltpu.VMEM((4 * width, model), F32),
        ],
        compiler_params=pltpu.CompilerParams(vmem_limit_bytes=56 << 20),
        cost_estimate=NO_COST,
    )(*waits, grad, h_one, weights, qkv, att, cosine, sine, start)


def gated(gate, up):
    logistic = jax.nn.sigmoid(gate)
    silu = gate * logistic
    return silu, silu * up, logistic * (1.0 + gate * (1.0 - logistic))


def routed_body(
    experts,
    rows_ref,
    up_ref,
    own_ref,
    router_ref,
    gate_w_ref,
    up_w_ref,
    down_w_ref,
    *rest,
):
    units_refs, rest = rest[:6], rest[6:]
    grad_rows_ref, grad_in_ref, high_ref, low_ref, row_gate_ref, total_ref, grads_ref, probs_ref, share_ref = rest
    part = pl.program_id(0)
    rows_in = rows_ref[...]
    each = rows_in.shape[0]
    here = pl.ds(pl.multiple_of(pl.program_id(1) * each, each), each)

    @pl.when(part == 0)
    def _():
        logits = dot(rows_in, router_ref[...], (1, 0))
        lane = lax.broadcasted_iota(jnp.int32, logits.shape, 1)
        logits = jnp.where(lane < experts, logits, -1e30)
        powers = jnp.exp(logits - jnp.max(logits, axis=1, keepdims=True))
        probs = powers / jnp.sum(powers, axis=1, keepdims=True)
        probs_ref[here] = probs
        gate = jnp.sum(probs * own_ref[...], axis=1, keepdims=True)
        row_gate_ref[...] = gate
        grad_rows = (gate * up_ref[...].astype(F32)).astype(BF)
        grad_rows_ref[...] = grad_rows
        grads_ref[here] = grad_rows

    gate_e = dot(rows_in, gate_w_ref[...], (1, 1))
    up_e = dot(rows_in, up_w_ref[...], (1, 1))
    silu, hidden, slope = gated(gate_e, up_e)
    hidden = hidden.astype(BF)
    grad_hidden = dot(grads_ref[here], down_w_ref[...], (1, 1))
    grad_gate = (grad_hidden * up_e * slope).astype(BF)
    grad_up = (grad_hidden * silu).astype(BF)
    for i in range(2):

        @pl.when(part == i)
        def _():
            for ref, made in zip(units_refs[3 * i :], (grad_gate, grad_up, hidden), strict=False):
                ref[...] = made

    share = jnp.sum(hidden.astype(F32) * grad_hidden, axis=1, keepdims=True)
    made = dot(grad_gate, gate_w_ref[...], (1, 0)) + dot(grad_up, up_w_ref[...], (1, 0))

    @pl.when(part == 0)
    def _():
        share_ref[here] = share
        total_ref[here] = made

    @pl.when(part > 0)
    def _():
        high, low = two_parts((share_ref[here] + share) * (own_ref[...] - probs_ref[here]))
        high_ref[...] = high
        low_ref[...] = low
        from_router = dot(high, router_ref[...], (1, 1)) + dot(low, router_ref[...], (1, 1))
        grad_in_ref[...] = (total_ref[here] + made + from_router).astype(BF)


def routed_expert(rows_in, up_rows, own, router, gate_w, up_w, down_w, experts, waits=()):
    total, model = rows_in.shape
    units = gate_w.shape[0]
    steps, parts = 2, 2
    each, part_units = total // steps, units // parts
    weight = pl.BlockSpec((part_units, model), lambda j, i: (j, 0))

    def by_rows(width, part=None):
        if part is None:
            return pl.BlockSpec((each, width), lambda j, i: (i, 0))
        if part == 0:
            return pl.BlockSpec((each, width), lambda j, i: (jnp.where(j == 0, i, steps - 1), 0))
        return pl.BlockSpec((each, width), lambda j, i: (jnp.where(j == 0, 0, i), 0))

    return pl.pallas_call(
        waiting(functools.partial(routed_body, experts), len(waits)),
        grid=(parts, steps),
        in_specs=[anywhere()] * len(waits)
        + [by_rows(model), by_rows(model), once_block(1, LANES), once_block(model, LANES)]
        + [weight] * 3,
        out_specs=[by_rows(part_units, 0)] * 3
        + [by_rows(part_units, 1)] * 3
        + [by_rows(model, 0), by_rows(model, 1)]
        + [by_rows(LANES, 1)] * 2
        + [by_rows(1, 0)],
        out_shape=[jax.ShapeDtypeStruct((total, part_units), BF)] * 6
        + [jax.ShapeDtypeStruct((total, model), BF)] * 2
        + [jax.ShapeDtypeStruct((total, LANES), BF)] * 2
        + [jax.ShapeDtypeStruct((total, 1), F32)],
        scratch_shapes=[
            pltpu.VMEM((total, model), F32),
            pltpu.VMEM((total, model), BF),
            pltpu.VMEM((total, LANES), F32),
            pltpu.VMEM((total, 1), F32),
        ],
        compiler_params=pltpu.CompilerParams(vmem_limit_bytes=60 << 20),
        cost_estimate=NO_COST,
    )(*waits, rows_in, up_rows, own, router, gate_w, up_w, down_w)


def routed_out_body(first_ref, second_ref, down_w_ref, row_gate_ref, out_ref):
    units = first_ref.shape[1]
    out = dot(first_ref[...], down_w_ref[:units], (1, 0))
    out += dot(second_ref[...], down_w_ref[units:], (1, 0))
    out_ref[...] = (row_gate_ref[...] * out.astype(BF).astype(F32)).astype(BF)


def routed_out(first, second, down_w, row_gate, waits=()):
    steps = 4
    total, model = first.shape[0], down_w.shape[1]
    each = model // steps
    return pl.pallas_call(
        waiting(routed_out_body, len(waits)),
        grid=(steps,),
        in_specs=[anywhere()] * len(waits)
        + [
            once_block(*first.shape),
            once_block(*second.shape),
            pl.BlockSpec((down_w.shape[0], each), lambda i: (0, i)),
            once_block(*row_gate.shape),
        ],
        out_specs=pl.BlockSpec((total, each), lambda i: (0, i)),
        out_shape=jax.ShapeDtypeStruct((total, model), BF),
        compiler_params=pltpu.CompilerParams(vmem_limit_bytes=40 << 20),
        cost_estimate=NO_COST,
    )(*waits, first, second, down_w, row_gate)


def shared_body(
    h_ref,
    up_ref,
    gate_up_w_ref,
    down_w_ref,
    mix_w_ref,
    kept_ref,
    given_ref,
    hidden_ref,
    grad_gate_ref,
    grad_up_ref,
    grad_out_ref,
    grad_mix_ref,
    mix_ref,
):
    units = down_w_ref.shape[0]
    h_in, mix_w = h_ref[...], mix_w_ref[...]
    mix = jax.nn.sigmoid(jnp.sum(h_in.astype(F32) * mix_w, axis=1, keepdims=True))
    mix_ref[...] = mix
    gate_s = dot(h_in, gate_up_w_ref[:units], (1, 1))
    up_s = dot(h_in, gate_up_w_ref[units:], (1, 1))
    silu, hidden, slope = gated(gate_s, up_s)
    hidden = hidden.astype(BF)
    hidden_ref[...] = hidden
    grad_out = (mix * up_ref[...].astype(F32)).astype(BF)
    grad_out_ref[...] = grad_out
    grad_hidden = dot(grad_out, down_w_ref[...], (1, 1))
    grad_gate = (grad_hidden * up_s * slope).astype(BF)
    grad_up = (grad_hidden * silu).astype(BF)
    grad_gate_ref[...] = grad_gate
    grad_up_ref[...] = grad_up
    grad_mix = jnp.sum(hidden.astype(F32) * grad_hidden, axis=1, keepdims=True) * (1.0 - mix)
    grad_mix_ref[...] = grad_mix
    made = dot(grad_gate, gate_up_w_ref[:units], (1, 0)) + dot(grad_up, gate_up_w_ref[units:], (1, 0))
    in_halves(kept_ref, given_ref, (made + grad_mix * mix_w).astype(BF))


def shared_expert(h_team, up_team, gate_up_w, down_w, mix_w, waits=()):
    total, model = h_team.shape
    units = down_w.shape[0]
    steps = 4
    each = total // steps
    return pl.pallas_call(
        waiting(shared_body, len(waits)),
        grid=(steps,),
        in_specs=[anywhere()] * len(waits)
        + [
            step_block(each, model),
            step_block(each, model),
            once_block(2 * units, model),
            once_block(units, model),
            once_block(1, model),
        ],
        out_specs=half_blocks(steps, each, model)
        + [step_block(each, units)] * 3
        + [step_block(each, model)]
        + [step_block(each, 1)] * 2,
        out_shape=[jax.ShapeDtypeStruct((total // 2, model), BF)] * 2
        + [jax.ShapeDtypeStruct((total, units), BF)] * 3
        + [jax.ShapeDtypeStruct((total, model), BF)]
        + [jax.ShapeDtypeStruct((total, 1), F32)] * 2,
        compiler_params=pltpu.CompilerParams(vmem_limit_bytes=56 << 20),
        cost_estimate=NO_COST,
    )(*waits, h_team, up_team, gate_up_w, down_w, mix_w)


def shared_out_body(hidden_ref, down_w_ref, mix_ref, kept_ref, given_ref):
    made = mix_ref[...] * dot(hidden_ref[...], down_w_ref[...], (1, 0))
    in_halves(kept_ref, given_ref, made.astype(BF))


def shared_out(hidden, down_w, mix, waits=()):
    total, units = hidden.shape
    model = down_w.shape[1]
    steps = 4
    each = total // steps
    return pl.pallas_call(
        waiting(shared_out_body, len(waits)),
        grid=(steps,),
        in_specs=[anywhere()] * len(waits)
        + [step_block(each, units), once_block(units, model), step_block(each, 1)],
        out_specs=half_blocks(steps, each, model),
        out_shape=[jax.ShapeDtypeStruct((total // 2, model), BF)] * 2,
        compiler_params=pltpu.CompilerParams(vmem_limit_bytes=40 << 20),
        cost_estimate=NO_COST,
    )(*waits, hidden, down_w, mix)


def nothing_body(*refs):
    del refs


def after(values_in, *others):
    return pl.pallas_call(
        nothing_body,
        in_specs=[anywhere()] * (1 + len(others)),
        out_specs=anywhere(),
        out_shape=jax.ShapeDtypeStruct(values_in.shape, values_in.dtype),
        input_output_aliases={0: 0},
        cost_estimate=NO_COST,
    )(values_in, *others)


def flip(values_in, axis, bit):
    size = lax.axis_size(axis)
    return lax.ppermute(values_in, axis, [(i, i ^ bit) for i in range(size)])


def shift(values_in, step):
    size = lax.axis_size(RING)
    return lax.ppermute(values_in, RING, [(i, (i + step) % size) for i in range(size)])


def shard_bits():
    bits, bit = [], lax.axis_size(SHARD) // 2
    while bit:
        bits.append(bit)
        bit //= 2
    return bits


def team_bits():
    bits = [(SHARD, bit) for bit in shard_bits()]
    return bits[:-1] + [(PAIR, 1)] + bits[-1:]


def team_order():
    order = [(0, 0)]
    for axis, bit in team_bits():
        order += [(p ^ bit, s) if axis == PAIR else (p, s ^ bit) for p, s in order]
    return order


def add_got(kept, given, axis, bit):
    return kept.astype(F32) + flip(given.astype(BF), axis, bit).astype(F32)


def halve(values_in, axis, bit):
    half = values_in.shape[0] // 2
    return add_got(values_in[:half], values_in[half:], axis, bit)


def team_sum(kept, given, held=None):
    bits = list(reversed(team_bits()))
    stages = [add_got(kept, given, *bits[0])]
    for i, (axis, bit) in enumerate(bits[1:]):
        ready = (held or {}).get(i, lambda: ())()
        stages.append(halve(after(stages[-1], *ready) if ready else stages[-1], axis, bit))
    return stages


def ring_gather(block):
    size = lax.axis_size(RING)
    ups, downs = [block], []
    up = down = block
    for k in range(1, size // 2 + 1):
        up = shift(up, 1)
        if k <= (size - 1) // 2:
            down = shift(down, -1)
            downs.append(down)
        ups.append(up)
        if k == 1 and downs:
            up = after(up, downs[0])
    return ups + downs


class RingSum:
    def __init__(self, blocks):
        size = lax.axis_size(RING)
        self.hops = size // 2
        self.back = list(blocks[1 : self.hops + 1])
        self.ahead = list(blocks[self.hops + 1 :])
        self.back_got = self.ahead_got = 0.0

    def running(self):
        back = [(self.back[-1].astype(F32) + self.back_got).astype(BF)]
        if len(self.back) == self.hops or not self.ahead:
            return back
        return back + [(self.ahead[-1].astype(F32) + self.ahead_got).astype(BF)]

    def hop(self, *ready):
        got = []
        for name, step, running in zip(("back", "ahead"), (-1, 1), self.running(), strict=False):
            getattr(self, name).pop()
            got.append(shift(after(running, *ready) if ready else running, step))
            setattr(self, name + "_got", got[-1].astype(F32))
        return got

    def total(self):
        while self.back or self.ahead:
            self.hop()
        return self.back_got + self.ahead_got


def ring_total(blocks):
    size = lax.axis_size(RING)
    total = blocks[0].astype(F32)
    if size > 4:
        others = RingSum(blocks).total()
        return total + others, (others,)
    offsets = [-k for k in range(1, size // 2 + 1)] + list(range(1, (size + 1) // 2))
    got = [shift(block, k) for k, block in zip(offsets, blocks[1:], strict=True)]
    return total + sum(one.astype(F32) for one in got), got


def pair_sum(own, other):
    return own.astype(F32) + flip(other.astype(BF), PAIR, 1).astype(F32)


def all_sum(values_in):
    for axis in (SHARD, PAIR, RING):
        bit = 1
        while bit < lax.axis_size(axis):
            values_in = values_in + flip(values_in, axis, bit)
            bit *= 2
    return values_in


def local(
    tokens,
    norm_attn,
    w_query,
    b_query,
    w_key,
    b_key,
    w_value,
    b_value,
    w_output,
    norm_ffn,
    w_router,
    shared_mix,
    shared_gate,
    shared_up,
    shared_down,
    expert_gate,
    expert_up,
    expert_down,
    routes,
    seq_lengths,
    cotangent,
):
    n_shard = lax.axis_size(SHARD)
    ring_at, pair_at, shard_at = (lax.axis_index(a) for a in (RING, PAIR, SHARD))
    expert_at = ring_at * 2 + pair_at
    group_rows, model = tokens.shape
    rows = group_rows // n_shard
    experts = w_router.shape[1]
    capacity = rows * TOP * 5 // (4 * experts)
    slot_rows = experts * capacity
    order = team_order()
    team = len(order)

    def block_of(values_in, flipped):
        return lax.dynamic_slice_in_dim(values_in, (shard_at ^ flipped) * rows, rows, 0)

    def halves(values_in):
        return values_in.reshape(2, values_in.shape[0] // 2, values_in.shape[1])

    def pair_units(parts):
        pack = jnp.concatenate([halves(part) for part in parts], axis=1)
        mine = lax.dynamic_index_in_dim(pack, pair_at, 0, keepdims=False)
        theirs = lax.dynamic_index_in_dim(pack, 1 - pair_at, 0, keepdims=False)
        got = flip(theirs, PAIR, 1)
        return jnp.where(
            pair_at == 0,
            jnp.concatenate([mine, got], axis=1),
            jnp.concatenate([got, mine], axis=1),
        )

    def gather_units(block):
        return lax.all_gather(block, RING, axis=1, tiled=True)

    def scatter_units(pack):
        return lax.psum_scatter(pack, RING, scatter_dimension=1, tiled=True)

    def unpair_units(summed, parts):
        width = summed.shape[1] // 2
        mine = lax.dynamic_slice_in_dim(summed, pair_at * width, width, 1)
        theirs = lax.dynamic_slice_in_dim(summed, (1 - pair_at) * width, width, 1)
        got = flip(theirs, PAIR, 1)
        first, second = jnp.where(pair_at == 0, mine, got), jnp.where(pair_at == 0, got, mine)
        n = summed.shape[0] // parts
        return [
            jnp.concatenate([first[i * n : (i + 1) * n], second[i * n : (i + 1) * n]], axis=0).astype(
                F32
            )
            for i in range(parts)
        ]

    attn_block = pair_units([w_query.T, w_key.T, w_value.T, w_output])
    attn_w = gather_units(attn_block)
    width_here = attn_w.shape[0] // 4
    heads_here = width_here // HD
    gate_up_block = pair_units([shared_gate.T, shared_up.T])
    down_block = pair_units([shared_down])

    shared_gate_up = gather_units(gate_up_block)
    shared_down_w = gather_units(down_block)

    def far_rows(block, hold=lambda i, joined: joined):
        far = [block]
        for i, bit in enumerate(shard_bits()):
            got = flip(hold(i, jnp.concatenate(far, axis=0)), SHARD, bit)
            far += [got[i * rows : (i + 1) * rows] for i in range(len(far))]
        return dict(zip([s for p, s in order if p == 1], far, strict=True))

    def team_rows(near, far):
        return jnp.concatenate([far[s] if p else near[s] for p, s in order], axis=0)

    near = {s: block_of(tokens, s) for p, s in order if p == 0}
    def shard_gather(parts):
        for bit in shard_bits()[1:]:
            parts = parts + [flip(one, SHARD, bit) for one in parts]
        return jnp.concatenate(parts, axis=0)

    first_bit = shard_bits()[0]
    far = far_rows(flip(near[0], PAIR, 1))
    gate_part = after(expert_gate[0].T, far[first_bit])
    gate_parts = [gate_part, flip(gate_part, SHARD, first_bit)]
    up_part = after(expert_up[0].T, gate_parts[1])
    up_parts = [up_part, flip(up_part, SHARD, first_bit)]
    gate_w, up_w = shard_gather(gate_parts), shard_gather(up_parts)
    tokens_team = team_rows(near, far)
    resid_in = near[0].astype(F32)

    ring_size = experts // 2
    slots = ring_size * capacity
    routes_in = jnp.concatenate(ring_gather(routes.T), axis=1)
    places = jnp.arange(ring_size * rows, dtype=jnp.int32)
    ahead = (jnp.arange(ring_size, dtype=jnp.int32) - ring_at + ring_size) % ring_size
    listed = jnp.where(
        ahead == 0, 0, jnp.where(ahead >= ring_size // 2, ring_size - ahead, ring_size // 2 + ahead)
    )

    def taking_of(expert):
        chosen = jnp.any(routes_in == expert, axis=0)
        slot = jnp.sum(
            jnp.where((places[None, :] < places[:, None]) & chosen[None, :], 1, 0), axis=1
        )
        slot = jnp.where(chosen, slot, -1)
        in_ring = jnp.take(slot.reshape(ring_size, rows), listed, axis=0).reshape(-1)
        ids = jnp.arange(slots, dtype=jnp.int32)[:, None]
        return (slot[None, :] == ids).astype(BF), (in_ring[None, :] == ids).astype(BF)

    take_own, take_own_up = taking_of(expert_at)
    take_other, take_other_up = taking_of(expert_at + 1 - 2 * pair_at)

    up_near = {s: block_of(cotangent, s) for p, s in order if p == 0}
    upstream = up_near[0].astype(F32)
    up_ring = lax.all_gather(after(up_near[0], attn_block), RING, axis=0, tiled=True)
    up_far = flip(up_near[0], PAIR, 1)
    up_own = dot(take_own_up, up_ring, (1, 0)).astype(BF)
    up_other = flip(dot(take_other_up, up_ring, (1, 0)).astype(BF), PAIR, 1)
    def team_gather(own, other, *ready):
        first = shard_bits()[0]
        both = jnp.concatenate([own, other], axis=0)
        got = flip(after(both, *ready) if ready else both, SHARD, first)
        rows_here = jnp.concatenate([own, got[:rows], other, got[rows:]], axis=0)
        return jnp.concatenate([rows_here, flip(rows_here, SHARD, shard_bits()[1])], axis=0)

    def shard_sums(kept, given):
        last, first = shard_bits()[-1], shard_bits()[0]
        summed = add_got(kept, given, SHARD, last)
        split = summed.reshape(2, 2, rows, model)
        sent = split[:, 1].astype(BF)
        done = add_got(split[:, 0], sent, SHARD, first)
        return sent, done.reshape(2 * rows, model)

    far_lengths = flip(seq_lengths, PAIR, 1)
    lengths = jnp.stack(
        [
            lax.dynamic_index_in_dim(far_lengths if p else seq_lengths, shard_at ^ s, 0, False)
            for p, s in order
        ]
    )
    positions = jax.vmap(lambda row: seq_positions(row, rows))(lengths)
    cosine, sine = (table.reshape(team * rows, HD) for table in rope_tables(positions, HD))
    start = (jnp.arange(rows, dtype=jnp.int32)[None, :] - positions).reshape(team * rows, 1)
    resid_team = tokens_team.astype(F32)
    gain_one = norm_attn.astype(F32)
    inv_one_team = lax.rsqrt(jnp.mean(resid_team * resid_team, axis=1, keepdims=True) + epsilon)
    h_one = (resid_team * inv_one_team * gain_one).astype(BF)
    head_start = (shard_at * 2 + pair_at) * width_here
    qkv_b = jnp.concatenate(
        [lax.dynamic_slice_in_dim(b, head_start, width_here, 0) for b in (b_query, b_key, b_value)]
    ).astype(F32)[None]
    attn_kept, attn_given, qkv, attended = attention_forward(
        h_one,
        attn_w,
        qkv_b,
        cosine,
        sine,
        start,
        rows,
        heads_here,
        ATTN_STEPS,
        (gate_parts[1], up_far, gate_up_block, down_block, take_own, take_other, take_own_up, take_other_up),
    )
    attn_out = team_sum(attn_kept, attn_given, {1: lambda: (up_parts[1],)})[-1]
    down_part = after(expert_down[0], attn_out)
    down_parts = [down_part, flip(down_part, SHARD, first_bit)]
    down_w = shard_gather(down_parts)

    up_far = far_rows(after(up_far, attn_out))
    up_team = team_rows(up_near, up_far)
    up_rows = jnp.concatenate([up_own, up_other], axis=0)

    x_two = resid_in + attn_out
    gain_two = norm_ffn.astype(F32)
    inv_two = lax.rsqrt(jnp.mean(x_two * x_two, axis=1, keepdims=True) + epsilon)
    h_two = (x_two * inv_two * gain_two).astype(BF)

    h_ring = ring_gather(h_two)
    h_team = team_gather(h_two, flip(h_two, PAIR, 1), h_ring[1], h_ring[-1])
    h_ring = after(jnp.concatenate(h_ring, axis=0), up_other, down_parts[1])
    rows_other = flip(dot(take_other, h_ring, (1, 0)).astype(BF), PAIR, 1)
    rows_in = jnp.concatenate([dot(take_own, h_ring, (1, 0)).astype(BF), rows_other], axis=0)

    own_expert = (jnp.arange(LANES, dtype=jnp.int32) == expert_at).astype(F32)[None]
    router_wide = jnp.pad(w_router, ((0, 0), (0, LANES - experts)))
    *units, grad_rows, grad_inputs, high, low, row_gate = routed_expert(
        rows_in, up_rows, own_expert, router_wide, gate_w, up_w, down_w, experts
    )
    kept_units, given_units = units[:3], units[3:]

    def returned(values_in, *ready):
        got = flip(values_in[slots:], PAIR, 1)
        own = after(values_in[:slots], *ready)
        made = (dot(take_own, own, (0, 0)) + dot(take_other, got, (0, 0))).astype(BF)
        return [made[i * rows : (i + 1) * rows] for i in range(ring_size)]

    def expert_products(units, across):
        return dot(units, across, (0, 0)).astype(BF)

    across = (rows_in, rows_in, grad_rows)

    mix_w = shared_mix.astype(F32)[None]
    (
        share_kept,
        share_given,
        hidden_s,
        grad_gate_s,
        grad_up_s,
        grad_out_s,
        grad_mix,
        mix_team,
    ) = shared_expert(
        h_team, up_team, shared_gate_up, shared_down_w, mix_w, (grad_inputs,)
    )
    grad_returned = returned(grad_inputs, share_given)

    def from_team(shared_rows):
        return pair_sum(shared_rows[:rows], shared_rows[rows:])

    share_stages = shard_sums(share_kept, share_given)
    grad_ring, ring_got = ring_total(grad_returned)
    grad_h_two = grad_ring + from_team(share_stages[-1])
    grad_x_two = norm_back(grad_h_two, x_two, inv_two, gain_two, upstream)
    grad_norm_ffn = jnp.sum(grad_h_two * x_two * inv_two, axis=0)

    grad_gate_s, grad_up_s, grad_out_s = (
        after(one, share_stages[0], *grad_returned[1:]) for one in (grad_gate_s, grad_up_s, grad_out_s)
    )
    shared_grad_pack = jnp.concatenate(
        [
            dot(grad_gate_s, h_team, (0, 0)).astype(BF),
            dot(grad_up_s, h_team, (0, 0)).astype(BF),
            dot(hidden_s, grad_out_s, (0, 0)).astype(BF),
        ],
        axis=0,
    )
    shared_grad_pack = after(shared_grad_pack, *ring_got, share_stages[-1])
    shared_summed = scatter_units(shared_grad_pack)
    mix_parts = jnp.concatenate(two_parts(grad_mix), axis=1)
    grad_mix_w = jnp.sum(dot(mix_parts, h_team, (0, 0)), axis=0)

    last_shard = shard_bits()[-1]
    ready = (shared_grad_pack,)
    expert_sums, given_grads = [], []
    for i in range(3):
        given_grads.append(expert_products(after(given_units[i], *ready), across[i]))
        kept = expert_products(after(kept_units[i], given_grads[-1]), across[i])
        expert_sums.append(add_got(kept, given_grads[-1], SHARD, last_shard))
        ready = (expert_sums[-1],)
        if i == 0:
            out_made = routed_out(kept_units[2], given_units[2], down_w, row_gate, ready)
            ready = (out_made,)
    out_kept, out_given = shared_out(hidden_s, shared_down_w, mix_team, ready)
    grad_router = (dot(high, rows_in, (0, 0)) + dot(low, rows_in, (0, 0)))[:experts]
    first, second, third = expert_sums
    grad_attn = grad_x_two.astype(BF)
    grad_other = flip(grad_attn, PAIR, 1)
    out_returned = returned(after(out_made, grad_other), grad_other)
    out_ring = RingSum(out_returned)
    out_ring.hop()
    grad_attn = team_gather(grad_attn, grad_other)
    units_half = first.shape[0] // 2
    sent = [one[units_half:].astype(BF) for one in (first, second, third)]
    sent = [after(one, grad_attn) for one in sent]
    grad_kept, grad_given, attn_grad_pack, grad_qkv_b = attention_backward(
        grad_attn, h_one, attn_w, qkv, attended, cosine, sine, start, rows, heads_here, ATTN_BACK_STEPS, (out_given, *sent, *out_returned[1:])
    )
    attn_grad_pack = after(attn_grad_pack, shared_summed)
    attn_summed = scatter_units(attn_grad_pack)
    grad_given = after(grad_given, attn_grad_pack)
    first, second, third = (
        add_got(after(one[:units_half], grad_kept), other, SHARD, first_bit)
        for one, other in zip((first, second, third), sent, strict=True)
    )
    grad_h_one = team_sum(
        grad_kept, grad_given, {0: lambda: (first, second, third)}
    )[-1]
    inv_one = lax.rsqrt(jnp.mean(resid_in * resid_in, axis=1, keepdims=True) + epsilon)
    grad_norm_attn = jnp.sum(grad_h_one * resid_in * inv_one, axis=0)
    grad_tokens = norm_back(grad_h_one, resid_in, inv_one, gain_one, grad_x_two)

    out_s = shard_sums(out_kept, after(out_given, attn_grad_pack))[-1]
    out_routed = out_returned[0].astype(F32) + out_ring.total()
    block_out = (x_two + out_routed + from_team(out_s)).astype(BF)

    grad_expert_gate, grad_expert_up, grad_expert_down = first, second, third
    grad_shared_gate, grad_shared_up, grad_shared_down = unpair_units(shared_summed, 3)
    grad_query_w, grad_key_w, grad_value_w, grad_output_w = unpair_units(attn_summed, 4)
    grad_qkv_b = lax.dynamic_update_slice_in_dim(
        jnp.zeros((3, b_query.shape[0]), F32), grad_qkv_b.reshape(3, width_here), head_start, 1
    )
    small = all_sum(
        jnp.concatenate(
            [
                grad_qkv_b,
                jnp.stack([grad_norm_attn, grad_norm_ffn, grad_mix_w]),
                grad_router,
            ],
            axis=0,
        )
    )
    return (
        block_out,
        grad_tokens,
        small[3],
        grad_query_w.T,
        small[0],
        grad_key_w.T,
        small[1],
        grad_value_w.T,
        small[2],
        grad_output_w,
        small[4],
        small[6:].T,
        small[5],
        grad_shared_gate.T,
        grad_shared_up.T,
        grad_shared_down,
        grad_expert_gate.T[None],
        grad_expert_up.T[None],
        grad_expert_down[None],
    )


def solution(mesh):
    experts, shards = mesh.shape["expert"], mesh.shape["shard"]
    grid = jax.sharding.Mesh(
        mesh.devices.reshape(experts // 2, 2, shards), (RING, PAIR, SHARD)
    )
    expert = (RING, PAIR)
    every = (RING, PAIR, SHARD)
    return jax.shard_map(
        local,
        mesh=grid,
        in_specs=(
            P(expert, None),
            P(),
            P(expert, SHARD),
            P(),
            P(expert, SHARD),
            P(),
            P(expert, SHARD),
            P(),
            P(SHARD, expert),
            P(),
            P(),
            P(),
            P(expert, SHARD),
            P(expert, SHARD),
            P(SHARD, expert),
            P(expert, None, SHARD),
            P(expert, None, SHARD),
            P(expert, SHARD, None),
            P(every, None),
            P(expert, None),
            P(expert, None),
        ),
        out_specs=(
            P(every, None),
            P(every, None),
            P(),
            P(expert, SHARD),
            P(),
            P(expert, SHARD),
            P(),
            P(expert, SHARD),
            P(),
            P(SHARD, expert),
            P(),
            P(),
            P(),
            P(expert, SHARD),
            P(expert, SHARD),
            P(SHARD, expert),
            P(expert, None, SHARD),
            P(expert, None, SHARD),
            P(expert, SHARD, None),
        ),
        check_vma=False,
    )
```

```python
import functools

import jax
import jax.numpy as jnp
from jax import lax
from jax.experimental import pallas as pl
from jax.experimental.pallas import tpu as pltpu
from jax.sharding import PartitionSpec as P

HD = 128
TOP = 4
LANES = 128


def taking(microseconds):
    return pl.CostEstimate(flops=int(microseconds * 1.15e9), bytes_accessed=0, transcendentals=0)

epsilon = 1e-06
rope_base = 1000000.0

RING, PAIR, SHARD = "ring", "pair", "shard"

BF, F32 = jnp.bfloat16, jnp.float32

ATTN_STEPS, ATTN_BACK_STEPS = 4, 2


def rope_tables(positions, head_size):
    exponent = jnp.arange(0, head_size, 2, dtype=F32) / head_size
    frequency = rope_base ** (-exponent)
    angles = positions.astype(F32)[..., None] * frequency
    cosine, sine = jnp.cos(angles), jnp.sin(angles)
    return jnp.concatenate([cosine, cosine, -sine, sine], axis=-1)


def seq_positions(lengths, length_total):
    seq_ends = jnp.cumsum(lengths)
    starts = seq_ends - lengths
    places = jnp.arange(length_total, dtype=jnp.int32)
    member = (places[:, None] >= starts[None, :]) & (places[:, None] < seq_ends[None, :])
    return places - jnp.sum(jnp.where(member, starts[None, :], 0), axis=1)


def norm_back(grad_normed, values_in, inverse, gain_wide, upstream_rows):
    normed = grad_normed * gain_wide
    return (
        upstream_rows
        + inverse * normed
        - values_in * inverse**3 * jnp.mean(normed * values_in, axis=1, keepdims=True)
    )


def dot(left, right, contract):
    return lax.dot_general(
        left, right, (((contract[0],), (contract[1],)), ((), ())), preferred_element_type=F32
    )


def two_parts(values_in):
    high = values_in.astype(BF)
    return high, (values_in - high.astype(F32)).astype(BF)


def from_table(table):
    return table[:, :HD], table[:, HD : 2 * HD], table[:, 2 * HD : 2 * HD + 1]


def swap_halves(values_in):
    return pltpu.roll(values_in, HD // 2, 1)


def causal_probs(query, key, start, scale):
    raw = dot(query, key, (1, 1)) * scale
    row = lax.broadcasted_iota(jnp.int32, raw.shape, 0)
    column = lax.broadcasted_iota(jnp.int32, raw.shape, 1)
    masked = jnp.where((column <= row) & (column.astype(F32) >= start), raw, -1e30)
    powers = jnp.exp(masked - jnp.max(masked, axis=-1, keepdims=True))
    return powers / jnp.sum(powers, axis=-1, keepdims=True)


def in_halves(kept_ref, given_ref, made):
    steps = pl.num_programs(0)

    @pl.when(pl.program_id(0) < steps // 2)
    def _():
        kept_ref[...] = made

    @pl.when(pl.program_id(0) >= steps // 2)
    def _():
        given_ref[...] = made


def half_blocks(steps, rows_each, width):
    half = steps // 2
    return [
        pl.BlockSpec((rows_each, width), lambda i: (jnp.minimum(i, half - 1), 0)),
        pl.BlockSpec((rows_each, width), lambda i: (jnp.maximum(i - half, 0), 0)),
    ]


def attention_forward_body(
    rows, heads, scale, h_ref, w_ref, bias_ref, table_ref, kept_ref, given_ref, qkv_ref, att_ref
):
    width = heads * HD
    qkv = dot(h_ref[...], w_ref[: 3 * width], (1, 1)) + bias_ref[...]
    for block in range(h_ref.shape[0] // rows):
        here = slice(block * rows, (block + 1) * rows)
        cosine, sine, start = from_table(table_ref[here])
        for head in range(heads):
            at = [slice(i * width + head * HD, i * width + (head + 1) * HD) for i in range(3)]
            query, key, value = (qkv[here, span] for span in at)
            query = (query * cosine + swap_halves(query) * sine).astype(BF)
            key = (key * cosine + swap_halves(key) * sine).astype(BF)
            value = value.astype(BF)
            for span, kept in zip(at, (query, key, value), strict=True):
                qkv_ref[here, span] = kept
            probs = causal_probs(query, key, start, scale).astype(BF)
            att_ref[here, at[0]] = dot(probs, value, (1, 0)).astype(BF)
    in_halves(kept_ref, given_ref, dot(att_ref[...], w_ref[3 * width :], (1, 0)).astype(BF))


def attention_backward_body(
    rows,
    heads,
    scale,
    first_ref,
    second_ref,
    h_ref,
    w_ref,
    qkv_ref,
    att_ref,
    table_ref,
    kept_ref,
    given_ref,
    pack_ref,
    bias_ref,
    grad_qkv_ref,
    total_ref,
):
    width = heads * HD
    step = pl.program_id(0)
    columns = first_ref.shape[1]
    grad_att = dot(first_ref[...], w_ref[3 * width :, :columns], (1, 1))
    grad_att += dot(second_ref[...], w_ref[3 * width :, columns:], (1, 1))
    grad_att = grad_att.astype(BF)
    for block in range(first_ref.shape[0] // rows):
        here = slice(block * rows, (block + 1) * rows)
        cosine, sine, start = from_table(table_ref[here])
        for head in range(heads):
            at = [slice(i * width + head * HD, i * width + (head + 1) * HD) for i in range(3)]
            query, key, value = (qkv_ref[here, span] for span in at)
            grad_out = grad_att[here, at[0]]
            probs = causal_probs(query, key, start, scale)
            grad_probs = dot(grad_out, value, (1, 1))
            grad_value = dot(probs.astype(BF), grad_out, (0, 0))
            delta = jnp.sum(probs * grad_probs, axis=-1, keepdims=True)
            grad_scores = (probs * (grad_probs - delta) * scale).astype(BF)
            grad_query = dot(grad_scores, key, (1, 0))
            grad_key = dot(grad_scores, query, (0, 0))
            grad_query = grad_query * cosine - swap_halves(grad_query) * sine
            grad_key = grad_key * cosine - swap_halves(grad_key) * sine
            for span, made in zip(at, (grad_query, grad_key, grad_value), strict=True):
                grad_qkv_ref[here, span] = made.astype(BF)
    grad_qkv = grad_qkv_ref[...]
    in_halves(kept_ref, given_ref, dot(grad_qkv, w_ref[: 3 * width], (1, 0)).astype(BF))
    bias_share = jnp.sum(grad_qkv.astype(F32), axis=0, keepdims=True)
    qkv_share = dot(grad_qkv, h_ref[...], (0, 0))
    out_first = dot(att_ref[...], first_ref[...], (0, 0))
    out_second = dot(att_ref[...], second_ref[...], (0, 0))

    @pl.when(step == 0)
    def _():
        bias_ref[...] = bias_share
        total_ref[: 3 * width] = qkv_share
        total_ref[3 * width :, :columns] = out_first
        total_ref[3 * width :, columns:] = out_second

    @pl.when(step > 0)
    def _():
        bias_ref[...] += bias_share
        total_ref[: 3 * width] += qkv_share
        total_ref[3 * width :, :columns] += out_first
        total_ref[3 * width :, columns:] += out_second

    @pl.when(step == pl.num_programs(0) - 1)
    def _():
        pack_ref[...] = total_ref[...].astype(BF)


def in_hbm(shape, dtype):
    return pltpu.HBM(shape, dtype)


def anywhere():
    return pl.BlockSpec(memory_space=pl.ANY)


def waiting(body, count):
    def run(*refs):
        body(*refs[count:])

    return run


def once_block(*shape):
    return pl.BlockSpec(shape, lambda *i: (0,) * len(shape), pipeline_mode=pl.Buffered(1))


def step_block(rows_each, *rest):
    return pl.BlockSpec((rows_each,) + rest, lambda i: (i,) + (0,) * len(rest))


def whole_block(*shape):
    return pl.BlockSpec(shape, lambda i: (0,) * len(shape))


def attention_forward(h_one, weights, bias, table, rows, heads, steps, waits=()):
    total, model = h_one.shape
    each, width = total // steps, heads * HD
    return pl.pallas_call(
        waiting(functools.partial(attention_forward_body, rows, heads, HD ** (-0.5)), len(waits)),
        grid=(steps,),
        in_specs=[anywhere()] * len(waits)
        + [
            step_block(each, model),
            whole_block(4 * width, model),
            whole_block(1, 3 * width),
            step_block(each, table.shape[1]),
        ],
        out_specs=half_blocks(steps, each, model) + [step_block(each, 3 * width), step_block(each, width)],
        out_shape=[
            in_hbm((total // 2, model), BF),
            in_hbm((total // 2, model), BF),
            in_hbm((total, 3 * width), BF),
            in_hbm((total, width), BF),
        ],
        compiler_params=pltpu.CompilerParams(vmem_limit_bytes=60 << 20),
        cost_estimate=taking(0),
    )(*waits, h_one, weights, bias, table)


def attention_backward(grads, h_one, weights, qkv, att, table, rows, heads, steps, waits=()):
    total, model = h_one.shape
    each, width = total // steps, heads * HD
    return pl.pallas_call(
        waiting(functools.partial(attention_backward_body, rows, heads, HD ** (-0.5)), len(waits)),
        grid=(steps,),
        in_specs=[anywhere()] * len(waits)
        + [
            step_block(each, model // 2),
            step_block(each, model // 2),
            step_block(each, model),
            whole_block(4 * width, model),
            step_block(each, 3 * width),
            step_block(each, width),
            step_block(each, table.shape[1]),
        ],
        out_specs=half_blocks(steps, each, model) + [whole_block(4 * width, model), whole_block(1, 3 * width)],
        out_shape=[
            in_hbm((total // 2, model), BF),
            in_hbm((total // 2, model), BF),
            in_hbm((4 * width, model), BF),
            in_hbm((1, 3 * width), F32),
        ],
        scratch_shapes=[
            pltpu.VMEM((each, 3 * width), BF),
            pltpu.VMEM((4 * width, model), F32),
        ],
        compiler_params=pltpu.CompilerParams(vmem_limit_bytes=60 << 20),
        cost_estimate=taking(35),
    )(*waits, *grads, h_one, weights, qkv, att, table)


def gated(gate, up):
    logistic = jax.nn.sigmoid(gate)
    silu = gate * logistic
    return silu, silu * up, logistic * (1.0 + gate * (1.0 - logistic))


def routed_body(experts, pieces, rows_ref, up_ref, own_ref, router_ref, *rest):
    weights, rest = rest[: 3 * pieces], rest[3 * pieces :]
    units_refs, rest = rest[:6], rest[6:]
    grad_rows_ref, grad_own_ref, grad_other_ref, high_ref, low_ref, row_gate_ref = rest[:6]
    total_ref, probs_ref, share_ref, all_ref, sem_ref = rest[6:]
    step, part = pl.program_id(0), pl.program_id(1)
    piece = weights[0].shape[0]
    half = pieces // 2
    copies = [
        [
            [
                pltpu.make_async_copy(
                    weights[kind * pieces + which * half + i],
                    all_ref.at[which, kind, pl.ds(i * piece, piece)],
                    sem_ref.at[kind * pieces + which * half + i],
                )
                for i in range(half)
            ]
            for kind in range(3)
        ]
        for which in range(2)
    ]

    @pl.when((step == 0) & (part == 0))
    def _():
        for one in sum(copies[0] + copies[1], []):
            one.start()

    def arrived(kind):
        for which in range(2):

            @pl.when((step == 0) & (part == which))
            def _():
                for one in copies[which][kind]:
                    one.wait()

        return all_ref[part, kind]

    rows_in = rows_ref[...]

    @pl.when(part == 0)
    def _():
        logits = dot(rows_in, router_ref[...], (1, 0))
        lane = lax.broadcasted_iota(jnp.int32, logits.shape, 1)
        logits = jnp.where(lane < experts, logits, -1e30)
        powers = jnp.exp(logits - jnp.max(logits, axis=1, keepdims=True))
        probs = powers / jnp.sum(powers, axis=1, keepdims=True)
        probs_ref[...] = probs

    gate = jnp.sum(probs_ref[...] * own_ref[...], axis=1, keepdims=True)
    grad_rows = (gate * up_ref[...].astype(F32)).astype(BF)

    @pl.when(part == 0)
    def _():
        row_gate_ref[...] = gate
        grad_rows_ref[...] = grad_rows

    gate_w = arrived(0)
    gate_e = dot(rows_in, gate_w, (1, 1))
    up_w = arrived(1)
    up_e = dot(rows_in, up_w, (1, 1))
    silu, hidden, slope = gated(gate_e, up_e)
    hidden = hidden.astype(BF)
    grad_hidden = dot(grad_rows, arrived(2), (1, 1))
    grad_gate = (grad_hidden * up_e * slope).astype(BF)
    grad_up = (grad_hidden * silu).astype(BF)
    for i in range(2):

        @pl.when(part == i)
        def _():
            for ref, made in zip(units_refs[3 * i :], (grad_gate, grad_up, hidden), strict=False):
                ref[...] = made

    share = jnp.sum(hidden.astype(F32) * grad_hidden, axis=1, keepdims=True)
    made = dot(grad_gate, gate_w, (1, 0)) + dot(grad_up, up_w, (1, 0))

    @pl.when(part == 0)
    def _():
        share_ref[...] = share
        total_ref[...] = made

    @pl.when(part > 0)
    def _():
        high, low = two_parts((share_ref[...] + share) * (own_ref[...] - probs_ref[...]))
        high_ref[...] = high
        low_ref[...] = low
        from_router = dot(high, router_ref[...], (1, 1)) + dot(low, router_ref[...], (1, 1))
        grad_in = (total_ref[...] + made + from_router).astype(BF)
        for i, ref in enumerate((grad_own_ref, grad_other_ref)):

            @pl.when(step == i)
            def _():
                ref[...] = grad_in


def routed_expert(rows_in, up_rows, own, router, weights, experts, waits=()):
    total, model = rows_in.shape
    pieces = len(weights[0])
    units = pieces * weights[0][0].shape[0]
    steps, parts = 2, 2
    each, part_units = total // steps, units // parts

    def by_rows(width):
        return pl.BlockSpec((each, width), lambda i, j: (i, 0))

    return pl.pallas_call(
        waiting(functools.partial(routed_body, experts, pieces), len(waits)),
        grid=(steps, parts),
        in_specs=[anywhere()] * len(waits)
        + [by_rows(model), by_rows(model), once_block(1, LANES), once_block(model, LANES)]
        + [anywhere()] * (3 * pieces),
        out_specs=[by_rows(part_units)] * 6
        + [by_rows(model)]
        + [once_block(each, model)] * 2
        + [by_rows(LANES)] * 2
        + [by_rows(1)],
        out_shape=[in_hbm((total, part_units), BF)] * 6
        + [in_hbm((total, model), BF)]
        + [in_hbm((each, model), BF)] * 2
        + [in_hbm((total, LANES), BF)] * 2
        + [in_hbm((total, 1), F32)],
        scratch_shapes=[
            pltpu.VMEM((each, model), F32),
            pltpu.VMEM((each, LANES), F32),
            pltpu.VMEM((each, 1), F32),
            pltpu.VMEM((parts, 3, part_units, model), BF),
            pltpu.SemaphoreType.DMA((3 * pieces,)),
        ],
        compiler_params=pltpu.CompilerParams(vmem_limit_bytes=60 << 20),
        cost_estimate=taking(20),
    )(*waits, rows_in, up_rows, own, router, *(one for kind in weights for one in kind))


def routed_out_body(pieces, first_ref, second_ref, row_gate_ref, *rest):
    weights, (own_ref, other_ref, down_ref) = rest[:pieces], rest[pieces:]
    piece = weights[0].shape[0]
    for i, ref in enumerate(weights):
        down_ref[i * piece : (i + 1) * piece] = ref[...]
    units = first_ref.shape[1]
    out = dot(first_ref[...], down_ref[:units], (1, 0))
    out += dot(second_ref[...], down_ref[units:], (1, 0))
    out = (row_gate_ref[...] * out.astype(BF).astype(F32)).astype(BF)
    own_ref[...] = out[: own_ref.shape[0]]
    other_ref[...] = out[own_ref.shape[0] :]


def routed_out(first, second, weights, row_gate, waits=()):
    steps = 4
    total, (piece, model) = first.shape[0], weights[0].shape
    each = model // steps
    return pl.pallas_call(
        waiting(functools.partial(routed_out_body, len(weights)), len(waits)),
        grid=(steps,),
        in_specs=[anywhere()] * len(waits)
        + [once_block(*first.shape), once_block(*second.shape), once_block(*row_gate.shape)]
        + [pl.BlockSpec((piece, each), lambda i: (0, i))] * len(weights),
        out_specs=[pl.BlockSpec((total // 2, each), lambda i: (0, i))] * 2,
        out_shape=[in_hbm((total // 2, model), BF)] * 2,
        scratch_shapes=[pltpu.VMEM((piece * len(weights), each), BF)],
        compiler_params=pltpu.CompilerParams(vmem_limit_bytes=60 << 20),
        cost_estimate=taking(7),
    )(*waits, first, second, row_gate, *weights)


def products_body(picks, stacked, units_refs_count, across_count, *refs):
    done_ref, refs = refs[-1], refs[:-1]
    done_ref[...] = jnp.zeros_like(done_ref)
    units_refs, refs = refs[:units_refs_count], refs[units_refs_count:]
    across_refs, out_refs = refs[:across_count], refs[across_count:]
    for i, (ref, pick) in enumerate(zip(units_refs, picks, strict=True)):
        made = dot(ref[...], across_refs[pick][...], (0, 0)).astype(BF)
        if stacked:
            rows = made.shape[0]
            out_refs[0][i * rows : (i + 1) * rows] = made
        else:
            out_refs[i][...] = made


def products(units, across, picks, stacked, waits=()):
    steps = 4
    rows, model = across[0].shape
    each, count = model // steps, units[0].shape[1]
    heights = [count * len(units)] if stacked else [count] * len(units)
    *made, done = pl.pallas_call(
        waiting(
            functools.partial(products_body, picks, stacked, len(units), len(across)), len(waits)
        ),
        grid=(steps,),
        in_specs=[anywhere()] * len(waits)
        + [once_block(rows, count)] * len(units)
        + [pl.BlockSpec((rows, each), lambda i: (0, i))] * len(across),
        out_specs=[pl.BlockSpec((height, each), lambda i: (0, i)) for height in heights]
        + [whole_block(8, LANES)],
        out_shape=[in_hbm((height, model), BF) for height in heights]
        + [in_hbm((8, LANES), F32)],
        compiler_params=pltpu.CompilerParams(vmem_limit_bytes=60 << 20),
        cost_estimate=taking(0.0045 * rows * len(units)),
    )(*waits, *units, *across)
    return made[0] if stacked else made, done


def shared_body(
    h_ref,
    up_ref,
    gate_up_w_ref,
    down_w_ref,
    mix_w_ref,
    kept_ref,
    given_ref,
    hidden_ref,
    grad_gate_ref,
    grad_up_ref,
    grad_out_ref,
    grad_mix_ref,
    mix_ref,
):
    units = down_w_ref.shape[0]
    h_in, mix_w = h_ref[...], mix_w_ref[...]
    mix = jax.nn.sigmoid(jnp.sum(h_in.astype(F32) * mix_w, axis=1, keepdims=True))
    mix_ref[...] = mix
    gate_s = dot(h_in, gate_up_w_ref[:units], (1, 1))
    up_s = dot(h_in, gate_up_w_ref[units:], (1, 1))
    silu, hidden, slope = gated(gate_s, up_s)
    hidden = hidden.astype(BF)
    hidden_ref[...] = hidden
    grad_out = (mix * up_ref[...].astype(F32)).astype(BF)
    grad_out_ref[...] = grad_out
    grad_hidden = dot(grad_out, down_w_ref[...], (1, 1))
    grad_gate = (grad_hidden * up_s * slope).astype(BF)
    grad_up = (grad_hidden * silu).astype(BF)
    grad_gate_ref[...] = grad_gate
    grad_up_ref[...] = grad_up
    grad_mix = jnp.sum(hidden.astype(F32) * grad_hidden, axis=1, keepdims=True) * (1.0 - mix)
    grad_mix_ref[...] = grad_mix
    made = dot(grad_gate, gate_up_w_ref[:units], (1, 0)) + dot(grad_up, gate_up_w_ref[units:], (1, 0))
    in_halves(kept_ref, given_ref, (made + grad_mix * mix_w).astype(BF))


def shared_expert(h_team, up_team, gate_up_w, down_w, mix_w, waits=()):
    total, model = h_team.shape
    units = down_w.shape[0]
    steps = 4
    each = total // steps
    return pl.pallas_call(
        waiting(shared_body, len(waits)),
        grid=(steps,),
        in_specs=[anywhere()] * len(waits)
        + [
            step_block(each, model),
            step_block(each, model),
            once_block(2 * units, model),
            once_block(units, model),
            once_block(1, model),
        ],
        out_specs=half_blocks(steps, each, model)
        + [step_block(each, units)] * 3
        + [step_block(each, model)]
        + [step_block(each, 1)] * 2,
        out_shape=[in_hbm((total // 2, model), BF)] * 2
        + [in_hbm((total, units), BF)] * 3
        + [in_hbm((total, model), BF)]
        + [in_hbm((total, 1), F32)] * 2,
        compiler_params=pltpu.CompilerParams(vmem_limit_bytes=60 << 20),
        cost_estimate=taking(34),
    )(*waits, h_team, up_team, gate_up_w, down_w, mix_w)


def shared_out_body(hidden_ref, down_w_ref, mix_ref, kept_ref, given_ref):
    made = mix_ref[...] * dot(hidden_ref[...], down_w_ref[...], (1, 0))
    in_halves(kept_ref, given_ref, made.astype(BF))


def shared_out(hidden, down_w, mix, waits=()):
    total, units = hidden.shape
    model = down_w.shape[1]
    steps = 4
    each = total // steps
    return pl.pallas_call(
        waiting(shared_out_body, len(waits)),
        grid=(steps,),
        in_specs=[anywhere()] * len(waits)
        + [step_block(each, units), once_block(units, model), step_block(each, 1)],
        out_specs=half_blocks(steps, each, model),
        out_shape=[in_hbm((total // 2, model), BF)] * 2,
        compiler_params=pltpu.CompilerParams(vmem_limit_bytes=60 << 20),
        cost_estimate=taking(6),
    )(*waits, hidden, down_w, mix)


def nothing_body(*refs):
    del refs


def after(values_in, *others):
    return pl.pallas_call(
        nothing_body,
        in_specs=[anywhere()] * (1 + len(others)),
        out_specs=anywhere(),
        out_shape=jax.ShapeDtypeStruct(values_in.shape, values_in.dtype),
        input_output_aliases={0: 0},
        cost_estimate=taking(0),
    )(values_in, *others)


def flip(values_in, axis, bit):
    size = lax.axis_size(axis)
    return lax.ppermute(values_in, axis, [(i, i ^ bit) for i in range(size)])


def shift(values_in, step):
    size = lax.axis_size(RING)
    return lax.ppermute(values_in, RING, [(i, (i + step) % size) for i in range(size)])


def shard_bits():
    bits, bit = [], lax.axis_size(SHARD) // 2
    while bit:
        bits.append(bit)
        bit //= 2
    return bits


def team_bits():
    bits = [(SHARD, bit) for bit in shard_bits()]
    return bits[:-1] + [(PAIR, 1)] + bits[-1:]


def team_order():
    order = [(0, 0)]
    for axis, bit in team_bits():
        order += [(p ^ bit, s) if axis == PAIR else (p, s ^ bit) for p, s in order]
    return order


def low_sum(parts):
    return sum(part.astype(F32) for part in parts).astype(BF)


def team_sum(kept, given, held):
    (_, last), _, (_, first) = reversed(team_bits())

    def arrive(got, stage):
        return after(got, *held[stage]) if stage in held else got

    parts = [kept, arrive(flip(given, SHARD, last), 0)]
    rows, columns = kept.shape[0] // 4, kept.shape[1] // 2
    sums = []
    for i, ways in enumerate((((PAIR, 1), (SHARD, first)), ((SHARD, first), (PAIR, 1)))):
        here = [part[:, i * columns : (i + 1) * columns].reshape(2, 2, rows, columns) for part in parts]
        if i:
            here = [part.swapaxes(0, 1) for part in here]
        for stage, way in enumerate(ways):
            got = flip(low_sum(part[1] for part in here), *way)
            here = [part[0] for part in here] + [arrive(got, stage + 1)]
        sums.append(sum(part.astype(F32) for part in here))
    return jnp.concatenate(sums, axis=1)


def ring_gather(block, *ready):
    size = lax.axis_size(RING)
    ups, downs = [block], []
    up = down = block
    for k in range(1, size // 2 + 1):
        up = shift(up, 1)
        if k <= (size - 1) // 2:
            down = shift(down, -1)
            downs.append(down)
        ups.append(up)
        if k == 1 and downs:
            up = after(up, downs[0], *ready)
    return ups + downs


class RingSum:
    def __init__(self, blocks):
        size = lax.axis_size(RING)
        self.hops = size // 2
        self.back = list(blocks[1 : self.hops + 1])
        self.ahead = list(blocks[self.hops + 1 :])
        self.back_got, self.ahead_got = [], []

    def hold(self, *ready):
        self.back_got = [after(one, *ready) for one in self.back_got]
        self.ahead_got = [after(one, *ready) for one in self.ahead_got]

    def hop(self, *ready):
        if ready:
            self.hold(*ready)
        both = len(self.back) < self.hops and self.ahead
        sent = [low_sum([self.back.pop()] + self.back_got)]
        if both:
            sent.append(low_sum([self.ahead.pop()] + self.ahead_got))
            self.ahead_got = [shift(sent[1], 1)]
        self.back_got = [shift(sent[0], -1)]
        return sent

    def total(self):
        while self.back or self.ahead:
            self.hop()
        return sum(one.astype(F32) for one in self.back_got + self.ahead_got)


def all_sum(values_in):
    for axis in (SHARD, PAIR, RING):
        bit = 1
        while bit < lax.axis_size(axis):
            values_in = values_in + flip(values_in, axis, bit)
            bit *= 2
    return values_in


def local(
    tokens,
    norm_attn,
    w_query,
    b_query,
    w_key,
    b_key,
    w_value,
    b_value,
    w_output,
    norm_ffn,
    w_router,
    shared_mix,
    shared_gate,
    shared_up,
    shared_down,
    expert_gate,
    expert_up,
    expert_down,
    routes,
    seq_lengths,
    cotangent,
):
    n_shard = lax.axis_size(SHARD)
    ring_at, pair_at, shard_at = (lax.axis_index(a) for a in (RING, PAIR, SHARD))
    expert_at = ring_at * 2 + pair_at
    group_rows, model = tokens.shape
    rows = group_rows // n_shard
    experts = w_router.shape[1]
    capacity = rows * TOP * 5 // (4 * experts)
    slot_rows = experts * capacity
    order = team_order()
    team = len(order)

    def block_of(values_in, flipped):
        return lax.dynamic_slice_in_dim(values_in, (shard_at ^ flipped) * rows, rows, 0)

    def halves(values_in):
        return values_in.reshape(2, values_in.shape[0] // 2, values_in.shape[1])

    def pair_units(parts, *ready):
        pack = jnp.concatenate([halves(part) for part in parts], axis=1)
        mine = lax.dynamic_index_in_dim(pack, pair_at, 0, keepdims=False)
        theirs = lax.dynamic_index_in_dim(pack, 1 - pair_at, 0, keepdims=False)
        got = flip(theirs, PAIR, 1)
        got = after(got, *ready) if ready else got
        return jnp.where(
            pair_at == 0,
            jnp.concatenate([mine, got], axis=1),
            jnp.concatenate([got, mine], axis=1),
        )

    def gather_units(block):
        return lax.all_gather(block, RING, axis=1, tiled=True)

    def scatter_units(pack):
        return lax.psum_scatter(pack, RING, scatter_dimension=1, tiled=True)

    def unpair_units(summed, parts):
        width = summed.shape[1] // 2
        mine = lax.dynamic_slice_in_dim(summed, pair_at * width, width, 1)
        theirs = lax.dynamic_slice_in_dim(summed, (1 - pair_at) * width, width, 1)
        got = flip(theirs, PAIR, 1)
        first, second = jnp.where(pair_at == 0, mine, got), jnp.where(pair_at == 0, got, mine)
        n = summed.shape[0] // parts
        return [
            jnp.concatenate([first[i * n : (i + 1) * n], second[i * n : (i + 1) * n]], axis=0).astype(
                F32
            )
            for i in range(parts)
        ]

    attn_block = pair_units([w_query.T, w_key.T, w_value.T, w_output])
    attn_w = gather_units(attn_block)
    width_here = attn_w.shape[0] // 4
    heads_here = width_here // HD
    def far_rows(block, hold=lambda i, joined: joined):
        far = [block]
        for i, bit in enumerate(shard_bits()):
            got = flip(hold(i, jnp.concatenate(far, axis=0)), SHARD, bit)
            far += [got[i * rows : (i + 1) * rows] for i in range(len(far))]
        return dict(zip([s for p, s in order if p == 1], far, strict=True))

    def team_rows(near, far):
        return jnp.concatenate([far[s] if p else near[s] for p, s in order], axis=0)

    near = {s: block_of(tokens, s) for p, s in order if p == 0}
    def shard_pieces(part):
        first_got = flip(part, SHARD, first_bit)
        parts = [part, first_got]
        return parts + [flip(one, SHARD, shard_bits()[1]) for one in parts], first_got

    first_bit = shard_bits()[0]
    far = far_rows(flip(near[0], PAIR, 1))

    gate_up_block = pair_units([shared_gate.T, shared_up.T], far[shard_bits()[1]])
    down_block = pair_units([shared_down], far[shard_bits()[1]])
    shared_gate_up = gather_units(gate_up_block)
    shared_down_w = gather_units(down_block)

    tokens_team = team_rows(near, far)
    resid_in = near[0].astype(F32)

    ring_size = experts // 2
    back = ring_size // 2
    nearer = [i for i in range(ring_size) if i != back]

    def whole_tiles(count):
        return -(-count // 16) * 16

    slots_near, slots_back = whole_tiles(capacity * (ring_size - 1)), whole_tiles(capacity)
    slots = slots_near + slots_back
    routes_in = jnp.concatenate(ring_gather(routes.T), axis=1)
    places = jnp.arange(ring_size * rows, dtype=jnp.int32)
    ahead = (jnp.arange(ring_size, dtype=jnp.int32) - ring_at + ring_size) % ring_size
    listed = jnp.where(
        ahead == 0, 0, jnp.where(ahead >= ring_size // 2, ring_size - ahead, ring_size // 2 + ahead)
    )

    def one_hot(slot, count):
        return (slot[None, :] == jnp.arange(count, dtype=jnp.int32)[:, None]).astype(BF)

    def taking_of(expert):
        chosen = jnp.any(routes_in == expert, axis=0)
        furthest = places // rows == back
        same = furthest[None, :] == furthest[:, None]
        earlier = (places[None, :] < places[:, None]) & same & chosen[None, :]
        slot = jnp.sum(earlier.astype(jnp.int32), axis=1) + jnp.where(furthest, slots_near, 0)
        slot = jnp.where(chosen, slot, -1)
        blocks = slot.reshape(ring_size, rows)
        in_ring = jnp.take(blocks, listed, axis=0).reshape(-1)
        near_slot = jnp.concatenate([blocks[i] for i in nearer])
        return (
            one_hot(slot, slots),
            one_hot(near_slot, slots_near),
            one_hot(blocks[back] - slots_near, slots_back),
            one_hot(in_ring, slots),
        )

    take_own, take_own_near, take_own_back, take_own_up = taking_of(expert_at)
    take_other, take_other_near, take_other_back, take_other_up = taking_of(
        expert_at + 1 - 2 * pair_at
    )

    up_near = {s: block_of(cotangent, s) for p, s in order if p == 0}
    upstream = up_near[0].astype(F32)
    up_ring = lax.all_gather(after(up_near[0], attn_block), RING, axis=0, tiled=True)
    up_far = far_rows(flip(up_near[0], PAIR, 1))
    up_team = team_rows(up_near, up_far)
    up_own = dot(take_own_up, up_ring, (1, 0)).astype(BF)
    up_other = flip(dot(take_other_up, up_ring, (1, 0)).astype(BF), PAIR, 1)
    def team_gather(own, other, ready, held, late):
        both = after(jnp.concatenate([own, other], axis=0), *ready)
        got = after(flip(both, SHARD, first_bit), *held)
        rows_here = jnp.concatenate([own, got[:rows], other, got[rows:]], axis=0)
        rows_here = after(rows_here, *late)
        return jnp.concatenate([rows_here, flip(rows_here, SHARD, shard_bits()[1])], axis=0)

    def team_spread(own, late):
        columns = own.shape[1] // 2
        one, two = own[:, :columns], own[:, columns:]
        across = flip(one, PAIR, 1)
        beside = flip(two, SHARD, first_bit)
        one_got = flip(jnp.concatenate([one, across], axis=0), SHARD, first_bit)
        two_got = flip(jnp.concatenate([two, beside], axis=0), PAIR, 1)
        one = [one, one_got[:rows], across, one_got[rows:]]
        two = [two, beside, two_got[:rows], two_got[rows:]]
        last = shard_bits()[1]
        halves_here = [jnp.concatenate(one, axis=0), jnp.concatenate(two, axis=0)]
        halves_here[1] = after(halves_here[1], *late)
        return [jnp.concatenate([half, flip(half, SHARD, last)], axis=0) for half in halves_here]

    def shard_sends(kept, given, *ready):
        got = flip(given, SHARD, shard_bits()[1])
        parts = [kept, after(got, *ready) if ready else got]
        parts = [part.reshape(2, 2, rows, model) for part in parts]
        sent = low_sum(part[:, 1] for part in parts)
        return sent, [part[:, 0] for part in parts]

    def shard_done(parts, got):
        return sum(part.astype(F32) for part in parts + [got]).reshape(2 * rows, model)

    far_lengths = flip(seq_lengths, PAIR, 1)
    lengths = jnp.stack(
        [
            lax.dynamic_index_in_dim(far_lengths if p else seq_lengths, shard_at ^ s, 0, False)
            for p, s in order
        ]
    )
    positions = jax.vmap(lambda row: seq_positions(row, rows))(lengths)
    start = (jnp.arange(rows, dtype=jnp.int32)[None, :] - positions).astype(F32)
    start = jnp.broadcast_to(start[..., None], (team, rows, LANES))
    table = jnp.concatenate([rope_tables(positions, HD), start], axis=-1).reshape(team * rows, -1)
    resid_team = tokens_team.astype(F32)
    gain_one = norm_attn.astype(F32)
    inv_one_team = lax.rsqrt(jnp.mean(resid_team * resid_team, axis=1, keepdims=True) + epsilon)
    h_one = (resid_team * inv_one_team * gain_one).astype(BF)
    head_start = (shard_at * 2 + pair_at) * width_here
    qkv_b = jnp.concatenate(
        [lax.dynamic_slice_in_dim(b, head_start, width_here, 0) for b in (b_query, b_key, b_value)]
    ).astype(F32)[None]
    attn_kept, attn_given, qkv, attended = attention_forward(
        h_one,
        attn_w,
        qkv_b,
        table,
        rows,
        heads_here,
        ATTN_STEPS,
        (up_far[shard_bits()[1]], gate_up_block, down_block, routes_in),
    )
    attn_out = team_sum(attn_kept, attn_given, {})

    gate_pieces, gate_got = shard_pieces(after(expert_gate[0].T, attn_out))
    up_pieces, up_got = shard_pieces(after(expert_up[0].T, attn_out))
    down_pieces, down_got = shard_pieces(after(expert_down[0], attn_out))

    up_rows = jnp.concatenate([up_own, up_other], axis=0)

    x_two = resid_in + attn_out
    gain_two = norm_ffn.astype(F32)
    inv_two = lax.rsqrt(jnp.mean(x_two * x_two, axis=1, keepdims=True) + epsilon)
    h_two = (x_two * inv_two * gain_two).astype(BF)

    h_ring = ring_gather(h_two)
    h_back = h_ring[back]
    h_near = jnp.concatenate([h_ring[i] for i in nearer], axis=0)
    near_got = flip(dot(take_other_near, h_near, (1, 0)).astype(BF), PAIR, 1)
    h_team = team_gather(
        h_two,
        after(flip(h_two, PAIR, 1), h_ring[1], h_ring[-1]),
        (gate_got, up_got, up_other, up_team),
        (near_got, down_got, h_back, up_rows),
        (shared_down_w,),
    )
    back_sent = dot(take_other_back, h_back, (1, 0)).astype(BF)
    back_got = after(flip(back_sent, PAIR, 1), h_team)
    rows_other = [near_got, back_got]
    rows_own = [
        dot(take_own_near, h_near, (1, 0)).astype(BF),
        dot(take_own_back, h_back, (1, 0)).astype(BF),
    ]
    rows_in = jnp.concatenate(rows_own + rows_other, axis=0)

    own_expert = (jnp.arange(LANES, dtype=jnp.int32) == expert_at).astype(F32)[None]
    router_wide = jnp.pad(w_router, ((0, 0), (0, LANES - experts)))
    *units, grad_rows, grad_in_own, grad_in_other, high, low, row_gate = routed_expert(
        rows_in,
        up_rows,
        own_expert,
        router_wide,
        (gate_pieces, up_pieces, down_pieces),
        experts,
    )
    kept_units, given_units = units[:3], units[3:]

    def returned(own, got):
        made = (dot(take_own, own, (0, 0)) + dot(take_other, got, (0, 0))).astype(BF)
        return [made[i * rows : (i + 1) * rows] for i in range(ring_size)]

    grad_got = flip(grad_in_other, PAIR, 1)
    out_own, out_other = routed_out(
        kept_units[2], given_units[2], down_pieces, row_gate, (grad_in_other, shared_gate_up)
    )

    mix_w = shared_mix.astype(F32)[None]
    (
        share_kept,
        share_given,
        hidden_s,
        grad_gate_s,
        grad_up_s,
        grad_out_s,
        grad_mix,
        mix_team,
    ) = shared_expert(
        h_team, up_team, shared_gate_up, shared_down_w, mix_w, (out_other,)
    )
    grad_returned = returned(after(grad_in_own, share_given), grad_got)

    def from_team(shared_rows):
        return shared_rows[:rows] + flip(shared_rows[rows:].astype(BF), PAIR, 1).astype(F32)

    share_sent, share_parts = shard_sends(share_kept, share_given, *grad_returned[1:2])
    share_got = flip(share_sent, SHARD, first_bit)
    grad_ring = RingSum(grad_returned)
    grad_ring.hop()

    shared_grad_pack, done = products(
        [grad_gate_s, grad_up_s, hidden_s],
        [h_team, grad_out_s],
        (0, 0, 1),
        True,
        (share_sent, *grad_returned[1:]),
    )
    next_sent = grad_ring.hop(done)
    given_grads, done = products(
        given_units, [rows_in, grad_rows], (0, 0, 1), False, (done, *next_sent)
    )
    grad_share = from_team(shard_done(share_parts, after(share_got, done)))
    kept_grads, done = products(kept_units, [rows_in, grad_rows], (0, 0, 1), False, (done,))
    grad_ring.hold(done)
    grad_h_two = grad_share + grad_returned[0].astype(F32) + grad_ring.total()
    grad_x_two = norm_back(grad_h_two, x_two, inv_two, gain_two, upstream)
    grad_norm_ffn = jnp.sum(grad_h_two * x_two * inv_two, axis=0)
    shared_summed = scatter_units(shared_grad_pack)
    mix_parts = jnp.concatenate(two_parts(grad_mix), axis=1)
    grad_mix_w = jnp.sum(dot(mix_parts, h_team, (0, 0)), axis=0)

    last_shard = shard_bits()[-1]
    ready = (shared_grad_pack,)
    grad_router = (dot(high, rows_in, (0, 0)) + dot(low, rows_in, (0, 0)))[:experts]
    grad_attn = grad_x_two.astype(BF)
    units_half = kept_grads[0].shape[0] // 2
    expert_parts = [
        [kept, flip(given, SHARD, last_shard)]
        for kept, given in zip(kept_grads, given_grads, strict=True)
    ]
    sent = [low_sum(part[units_half:] for part in parts) for parts in expert_parts]
    grad_attn = team_spread(grad_attn, sent)
    first_got, second_got, third_got = (
        flip(after(one, *grad_attn), SHARD, first_bit) for one in sent
    )
    out_got = flip(after(out_other, *grad_attn), PAIR, 1)
    grad_kept, grad_given, attn_grad_pack, grad_qkv_b = attention_backward(
        grad_attn, h_one, attn_w, qkv, attended, table, rows, heads_here, ATTN_BACK_STEPS, (out_own,)
    )
    attn_grad_pack = after(attn_grad_pack, shared_summed)
    attn_summed = scatter_units(attn_grad_pack)
    out_kept, out_given = shared_out(hidden_s, shared_down_w, mix_team, (grad_kept,))
    out_sent, out_parts = shard_sends(out_kept, out_given)
    out_shard_got = flip(out_sent, SHARD, first_bit)
    first_got, second_got = (after(one, grad_kept) for one in (first_got, second_got))
    third_got, out_got, out_shard_got = (
        after(one, attn_grad_pack) for one in (third_got, out_got, out_shard_got)
    )
    out_returned = returned(out_own, out_got)
    out_ring = RingSum(out_returned)
    out_ring.hop()
    grad_h_one = team_sum(
        grad_kept,
        grad_given,
        {0: (attn_grad_pack, first_got, second_got), 2: (third_got, *out_returned[1:])},
    )
    grad_expert_gate, grad_expert_up, grad_expert_down = (
        sum(part[:units_half].astype(F32) for part in parts) + got.astype(F32)
        for parts, got in zip(expert_parts, (first_got, second_got, third_got), strict=True)
    )
    inv_one = lax.rsqrt(jnp.mean(resid_in * resid_in, axis=1, keepdims=True) + epsilon)
    grad_norm_attn = jnp.sum(grad_h_one * resid_in * inv_one, axis=0)
    grad_tokens = norm_back(grad_h_one, resid_in, inv_one, gain_one, grad_x_two)

    out_s = shard_done(out_parts, out_shard_got)
    out_routed = out_returned[0].astype(F32) + out_ring.total()
    block_out = (x_two + out_routed + from_team(out_s)).astype(BF)

    grad_shared_gate, grad_shared_up, grad_shared_down = unpair_units(shared_summed, 3)
    grad_query_w, grad_key_w, grad_value_w, grad_output_w = unpair_units(attn_summed, 4)
    grad_qkv_b = lax.dynamic_update_slice_in_dim(
        jnp.zeros((3, b_query.shape[0]), F32), grad_qkv_b.reshape(3, width_here), head_start, 1
    )
    small = all_sum(
        jnp.concatenate(
            [
                grad_qkv_b,
                jnp.stack([grad_norm_attn, grad_norm_ffn, grad_mix_w]),
                grad_router,
            ],
            axis=0,
        )
    )
    return (
        block_out,
        grad_tokens,
        small[3],
        grad_query_w.T,
        small[0],
        grad_key_w.T,
        small[1],
        grad_value_w.T,
        small[2],
        grad_output_w,
        small[4],
        small[6:].T,
        small[5],
        grad_shared_gate.T,
        grad_shared_up.T,
        grad_shared_down,
        grad_expert_gate.T[None],
        grad_expert_up.T[None],
        grad_expert_down[None],
    )


def solution(mesh):
    experts, shards = mesh.shape["expert"], mesh.shape["shard"]
    grid = jax.sharding.Mesh(
        mesh.devices.reshape(experts // 2, 2, shards), (RING, PAIR, SHARD)
    )
    expert = (RING, PAIR)
    every = (RING, PAIR, SHARD)
    return jax.shard_map(
        local,
        mesh=grid,
        in_specs=(
            P(expert, None),
            P(),
            P(expert, SHARD),
            P(),
            P(expert, SHARD),
            P(),
            P(expert, SHARD),
            P(),
            P(SHARD, expert),
            P(),
            P(),
            P(),
            P(expert, SHARD),
            P(expert, SHARD),
            P(SHARD, expert),
            P(expert, None, SHARD),
            P(expert, None, SHARD),
            P(expert, SHARD, None),
            P(every, None),
            P(expert, None),
            P(expert, None),
        ),
        out_specs=(
            P(every, None),
            P(every, None),
            P(),
            P(expert, SHARD),
            P(),
            P(expert, SHARD),
            P(),
            P(expert, SHARD),
            P(),
            P(SHARD, expert),
            P(),
            P(),
            P(),
            P(expert, SHARD),
            P(expert, SHARD),
            P(SHARD, expert),
            P(expert, None, SHARD),
            P(expert, None, SHARD),
            P(expert, SHARD, None),
        ),
        check_vma=False,
    )
```
